32 devices in a mesh: mem: 4 (over y, x), tile: 8 (over z, core).
Axes of the slice: x: 2, y: 2, z: 4, core: 2. Of those that a mesh axis runs over, the one named last changes fastest.
Arguments:
- alpha: float32 [8, 32, 128, 128], P('mem', None, 'tile'), may hold values from -6 to 6
- members: bfloat16 [8, 2, 32, 128, 128], P('mem', None, None, 'tile'), may hold values from -5 to 5
- scales: float32 [32], replicated, may hold values from 4 to 256
- observed: float32 [256, 256], P('tile'), may hold values from -6 to 6
- precision: float32 [256, 256], P('tile'), may hold values from 0.5 to 4
- ray_weights: float32 [256, 2, 256], P('tile'), may hold values from -1 to 1
- cell_index: int32 [256, 256], P('tile'), may hold values from 0 to 65535
- owner: int32 [256, 1], P('tile'), may hold values from 0 to 7; in each aligned block of 32 rows (0 to 31, 32 to 63, ...) at most 12 rows name the same one
Outputs:
- gradient: float32 [8, 32, 128, 128], P('mem', None, 'tile')
The draws below stay inside these ranges and needn't reach their ends.
Inputs may be any that keep to these rules, and one draw needn't show every extreme that they name: Among the rays of one strip, at most 12 name the same owner, and in every draw some strip sends exactly 12 rays to one owner. `cell_index`: A gate's index refers to a cell of the strip named by owner.
All inputs are finite; a program needn't handle non-finite values.
Results may differ from the reference program's by a relative error of at most 0.0003.
Values sent between devices are 32-bit elements; how exact they have to be, the bound alone decides.
No kernel may reach another device: no remote copies, remote signals or barrier semaphores. Data moves between devices by JAX's collectives and lax.ppermute only.
A program may use at most 192 MiB of HBM per device.

```python
import math
import jax
import jax.numpy as jnp
import numpy as np
from jax import lax

TX = 16
NY = 128
LEV = 32
G = 256
R_DEV = 32
MEM = 8
TILES = 8
NX = 128
RAYS = 256
CAP = 12
CELLS = 65536


def plant(result, key, low, largest):
    spot = [jax.random.randint(jax.random.fold_in(key, axis), (), 0, length) for axis, length in enumerate(result.shape)]
    main_axis = result.shape.index(max(result.shape))
    next_to = spot[:main_axis] + [(spot[main_axis] + 1) % result.shape[main_axis]] + spot[main_axis + 1:]
    return result.at[tuple(spot)].set(low).at[tuple(next_to)].set(largest)


def block_scale(rng, extent, cuts, least, largest):
    def one(dim, shards_of):
        heights = jax.random.uniform(jax.random.fold_in(jax.random.fold_in(rng, 6), dim), (shards_of,), jnp.float32, least / len(cuts), largest / len(cuts))
        return jnp.repeat(jnp.exp(heights), extent[dim] // shards_of).reshape((-1,) + (1,) * (len(extent) - dim - 1))

    level = one(*cuts[0])
    for cut in cuts[1:]:
        level = level * one(*cut)
    return level


def assign_block(stream_key, own, number, rows, number_of, top, most, skew):
    sequence = jax.random.permutation(stream_key, number_of)
    packed, common = shares(number_of, rows * top, most, skew, True), shares(number_of, rows * top, most, skew, False)
    places = jnp.arange(number_of)

    def named(tallies, offset_by):
        used = int((tallies > 0).sum())
        fixed = max(1, used // 4)
        passed = fixed + (places - fixed + offset_by * (used - fixed)) % max(1, number_of - fixed)
        return jnp.zeros((number_of,), jnp.int32).at[sequence[jnp.where(places < fixed, places, passed)]].set(jnp.asarray(tallies, jnp.int32))

    tallies = jnp.where(number % 4 == 0, named(packed, number // 4), named(common, number - number // 4 - 1))
    mixed = jax.random.permutation(jax.random.fold_in(own, 3), number_of)
    donor, taker = mixed[0:number_of // 2 * 2:2], mixed[1:number_of // 2 * 2:2]
    room = jnp.minimum(tallies[donor] - 1, most - tallies[taker]) // 2
    room = jnp.where((donor == sequence[0]) | (taker == sequence[0]) | (tallies[taker] == 0), 0, jnp.maximum(room, 0))
    passed = jax.random.randint(jax.random.fold_in(own, 4), (number_of // 2,), 0, 1 << 20) % (room + 1)
    tallies = tallies.at[donor].add(-passed).at[taker].add(passed)
    items = jnp.searchsorted(jnp.cumsum(tallies), jnp.arange(rows * top), side="right").astype(jnp.int32)
    grid = items.reshape(top, rows).T
    grid = grid[jax.random.permutation(jax.random.fold_in(own, 1), rows)]
    offset_by = jax.random.randint(jax.random.fold_in(own, 2), (rows, 1), 0, top)
    return jnp.take_along_axis(grid, (jnp.arange(top)[None, :] + offset_by) % top, axis=1)


def shares(amount, total, most, skew, full):
    loads = [(1 << 20) // math.isqrt(rank ** skew) + 1 for rank in range(1, amount + 1)]
    largest = most if full else min(most, max(-(-total // amount), total * loads[0] // sum(loads)))
    least = 1 if total - largest >= amount - 1 else 0
    counts, rest = [largest] + [least] * (amount - 1), total - largest - least * (amount - 1)
    while rest > 0:
        candidates = [i for i in range(1, amount) if counts[i] < largest] or [i for i in range(1, amount) if counts[i] < most]
        whole, remaining = sum([loads[i] for i in candidates]), rest
        for i in candidates:
            more = min(most - counts[i], max(1, remaining * loads[i] // whole), rest)
            counts[i] = counts[i] + more
            rest = rest - more
    return np.array(counts)


def scatter_about(own_key, dims, width, most, shards=(), held_as=jnp.bfloat16):
    entries = jax.random.normal(own_key, dims, jnp.float32) * width
    if len(shards) > 0:
        entries = block_scale(own_key, dims, shards, -0.22, 0.18) * entries
    return jnp.clip(entries, min=-most, max=most).astype(held_as)


def setup_inputs(seed: int = 0) -> dict:
    splits = jax.random.split(jax.random.key(seed), 9)
    alpha = scatter_about(splits[0], (MEM, LEV, NX, NY), 1.0, 6.0, ((0, 4), (2, 8)), jnp.float32)
    members = scatter_about(splits[1], (MEM, 2, LEV, NX, NY), 0.35, 5.0, ((0, 4), (3, 8)))
    scales = jnp.clip(jnp.exp(jax.random.uniform(splits[2], (LEV,), jnp.float32, math.log(4.0), math.log(256.0))), 4.0, 256.0)
    observed = scatter_about(splits[3], (RAYS, G), 1.0, 6.0, ((0, 8),), jnp.float32)
    precision = jnp.clip(jnp.exp(math.log(4.0) - 2.0794415 * jax.random.uniform(splits[4], (RAYS, G), jnp.float32) ** block_scale(splits[4], (RAYS, G), ((0, 8),), -0.2, 0.2)), 0.5, 4.0)
    ray_weights = jnp.clip(jax.random.uniform(splits[5], (RAYS, 2, G), jnp.float32, -1.0, 1.0) * block_scale(splits[5], (RAYS, 2, G), ((0, 8),), -0.4, 0.0), -1.0, 1.0)
    cell_index = plant(jax.random.randint(splits[6], (RAYS, G), 0, CELLS), jax.random.fold_in(splits[6], 1), 0, CELLS - 1).astype(jnp.int32)
    owner_keys = jax.random.split(jax.random.fold_in(splits[7], 1), RAYS // R_DEV)
    owner_turns = jax.random.permutation(jax.random.fold_in(splits[7], 3), RAYS // R_DEV)
    owner = jax.vmap(lambda own, number: assign_block(jax.random.fold_in(splits[7], 2), own, number, R_DEV, TILES, 1, CAP, 2))(owner_keys, owner_turns).reshape((RAYS, 1))
    return {"alpha": alpha, "members": members, "scales": scales, "observed": observed, "precision": precision, "ray_weights": ray_weights, "cell_index": cell_index, "owner": owner}


def kernel(log_rate, count):
    pos = jnp.arange(count).astype(jnp.float32)
    dist = jnp.abs(pos[:, None] - pos[None, :])
    top = jnp.maximum(pos[:, None], pos[None, :])
    rate = log_rate[:, None, None]
    decay = jnp.exp(rate)
    norm = jnp.sqrt((1.0 + decay) * -jnp.expm1(rate)) / (1.0 + decay)
    return norm * jnp.exp(rate * dist) * -jnp.expm1(2.0 * rate * (count - top))

def localize(field, kx, ky, kz):
    hp = lax.Precision.HIGHEST
    field = jnp.einsum('kl,lxy->kxy', kz, field, precision=hp)
    field = jnp.einsum('lyz,lxz->lxy', ky, field, precision=hp)
    return jnp.einsum('lxw,lwy->lxy', kx, field, precision=hp)

def reference(alpha, members, scales, observed, precision, ray_weights, cell_index, owner):
    rate = -1.0 / scales
    kx = kernel(rate, NX)
    ky = kernel(rate, NY)
    kz = kernel(jnp.full((1,), -1.0 / 3.0, jnp.float32), LEV)[0]

    def add_member(total, item):
        weight, member = item
        smooth = localize(weight, kx, ky, kz)
        return (total + member.astype(jnp.float32) * smooth[None], None)
    start = jnp.zeros((2, LEV, NX, NY), jnp.float32)
    increment, _ = lax.scan(add_member, start, (alpha, members))
    flat = increment.reshape(2, -1)
    level = cell_index // (TX * NY)
    row = cell_index // NY % TX + owner * TX
    column = cell_index % NY
    where = (level * (NX * NY) + row * NY + column).astype(jnp.int32)
    modelled = ray_weights[:, 0] * flat[0][where] + ray_weights[:, 1] * flat[1][where]
    departure = precision * (modelled - observed)
    places = where.reshape(-1)
    adjoint_u = jnp.zeros((LEV * NX * NY,), jnp.float32).at[places].add((ray_weights[:, 0] * departure).reshape(-1))
    adjoint_v = jnp.zeros((LEV * NX * NY,), jnp.float32).at[places].add((ray_weights[:, 1] * departure).reshape(-1))
    adjoint = jnp.stack([adjoint_u, adjoint_v]).reshape(2, LEV, NX, NY)

    def one_member(item):
        weight, member = item
        mixed = lax.optimization_barrier(jnp.sum(member.astype(jnp.float32) * adjoint, axis=0))
        return weight + localize(mixed, kx, ky, kz)
    return lax.map(one_member, (alpha, members))
```

```python
import functools
import math

import jax
import jax.numpy as jnp
from jax import lax
from jax.experimental import pallas as pl
from jax.experimental.pallas import tpu as pltpu
from jax.sharding import PartitionSpec as P

F32 = jnp.float32
BF16 = jnp.bfloat16
I32 = jnp.int32
LANES = 128
FIELDS = 5
Z_DECAY = math.exp(-1.0 / 3.0)
Z_GAIN = (1.0 - Z_DECAY) ** 2 * math.sqrt((1.0 + Z_DECAY) / (1.0 - Z_DECAY))
VMEM = pl.BlockSpec(memory_space=pltpu.VMEM)
PARAMS = pltpu.CompilerParams(vmem_limit_bytes=48 * 1024 * 1024)


def split(x):
    high = x.astype(BF16)
    return high, (x - high.astype(F32)).astype(BF16)


def dot(a, b):
    return jnp.dot(a, b, preferred_element_type=F32)


def dot3(a, b):
    (ah, al), (bh, bl) = split(a), split(b)
    return dot(ah, bh) + (dot(ah, bl) + dot(al, bh))


def iota(shape, dim):
    return lax.broadcasted_iota(I32, shape, dim)


def norm_of(rate):
    x = -rate
    series = jnp.ones_like(x)
    for k in (8, 7, 6, 5, 4, 3, 2):
        series = 1.0 - series * x * (1.0 / k)
    return jnp.sqrt(x * series / (1.0 + jnp.exp(rate)))


def pack_rays_kernel(tiles, per, owner_ref, cell_ref, weights_ref, observed_ref, precision_ref, *outs):
    rays, gates = observed_ref.shape
    halves = gates // LANES
    place, part = lax.axis_index("tile"), lax.axis_index("mem")
    owner = owner_ref[...]
    named = (owner == iota((rays, LANES), 1)).astype(F32)
    earlier = (iota((rays, rays), 0) > iota((rays, rays), 1)).astype(F32)
    rank = jnp.sum(dot(earlier, named) * named, axis=1, keepdims=True).astype(I32)
    step = lax.rem(owner - place + tiles, tiles)
    column = iota((rays, LANES), 1)
    target, row = column // per, column % per + part * per
    picks = [
        ((step == target) & (rank * halves + half == row)).astype(F32).T[: tiles * per]
        for half in range(halves)
    ]
    fields = (
        cell_ref[...].astype(F32),
        weights_ref[:, 0, :],
        weights_ref[:, 1, :],
        observed_ref[...],
        precision_ref[...],
    )
    for f, field in enumerate(fields):
        got = sum(
            jnp.dot(
                picks[half],
                field[:, half * LANES : (half + 1) * LANES],
                precision=lax.Precision.HIGHEST,
                preferred_element_type=F32,
            )
            for half in range(halves)
        )
        for k in range(tiles):
            outs[k][f] = got[k * per : (k + 1) * per]


def filter_levels(field_ref, out_ref):
    levels = field_ref.shape[1]
    state = field_ref[:, 0]
    out_ref[:, 0] = state
    for l in range(1, levels):
        state = field_ref[:, l] + Z_DECAY * state
        out_ref[:, l] = state
    for l in range(levels - 2, -1, -1):
        state = out_ref[:, l] + Z_DECAY * state
        out_ref[:, l] = state


def filter_columns(field_ref, high_ref, low_ref, out_ref):
    members, levels, rows, columns = field_ref.shape

    def level(l, _):
        field = field_ref[:, l].reshape(members * rows, columns)
        high, low = split(field)
        both = dot(jnp.concatenate([high, low], axis=0), high_ref[l])
        total = both[: members * rows] + (both[members * rows :] + dot(high, low_ref[l]))
        out_ref[:, l] = total.reshape(members, rows, columns)
        return 0

    lax.fori_loop(0, levels, level, 0, unroll=4)


def columns_matrix(rate_ref, high_ref, low_ref):
    levels, n, _ = high_ref.shape
    i, j = iota((n, n), 0), iota((n, n), 1)
    dist = jnp.abs(i - j).astype(F32)
    left = (2 * (n - jnp.maximum(i, j))).astype(F32)

    def level(l, _):
        rate = rate_ref[pl.ds(l, 1), :]
        matrix = (Z_GAIN * norm_of(rate)) * jnp.exp(rate * dist) * (1.0 - jnp.exp(rate * left))
        high_ref[l], low_ref[l] = split(matrix)
        return 0

    lax.fori_loop(0, levels, level, 0, unroll=2)


def states(tiles, rate_ref, field_ref, outs):
    members, levels, rows, columns = field_ref.shape
    place = lax.axis_index("tile")
    per = LANES // rows
    level, column = iota((per, LANES), 0), iota((per, LANES), 1)
    same = level == column // rows
    at = (column % rows).astype(F32)
    left = (2 * (rows * tiles - rows * place) - 2 * (column % rows)).astype(F32)
    for g in range(levels // per):
        rate = rate_ref[g * per : (g + 1) * per]
        norm = norm_of(rate)
        forward = jnp.where(same, norm * jnp.exp(rate * (rows - 1.0 - at)), 0.0)
        backward = jnp.where(same, norm * jnp.exp(rate * at) * (1.0 - jnp.exp(rate * left)), 0.0)
        both = jnp.concatenate([forward, backward], axis=0)
        for b in range(members):
            field = field_ref[b, g * per : (g + 1) * per].reshape(per * rows, columns)
            got = dot3(both, field)
            for k in range(1, tiles):
                outs[k - 1][b, g * per : (g + 1) * per] = jnp.where(place + k < tiles, got[:per], got[per:])


def first_kernel(tiles, rate_ref, alpha_ref, high_ref, low_ref, out_ref, *rest):
    outs, scratch = rest[:-1], rest[-1]
    columns_matrix(rate_ref, high_ref, low_ref)
    filter_levels(alpha_ref, scratch)
    filter_columns(scratch, high_ref, low_ref, out_ref)
    states(tiles, rate_ref, out_ref, outs)


def within_kernel(tiles, rate_ref, field_ref, out_ref):
    members, levels, rows, columns = field_ref.shape
    place = lax.axis_index("tile")
    per = LANES // rows
    n = per * rows
    row, column = iota((n, n), 0), iota((n, n), 1)
    same = row // rows == column // rows
    i, j = row % rows, column % rows
    dist = jnp.abs(i - j).astype(F32)
    left = (2 * (rows * tiles - rows * place) - 2 * jnp.maximum(i, j)).astype(F32)
    for g in range(levels // per):
        rate = jnp.concatenate(
            [jnp.broadcast_to(rate_ref[l : l + 1], (rows, LANES)) for l in range(g * per, (g + 1) * per)], axis=0
        )
        matrix = jnp.where(same, norm_of(rate) * jnp.exp(rate * dist) * (1.0 - jnp.exp(rate * left)), 0.0)
        for b in range(members):
            field = field_ref[b, g * per : (g + 1) * per].reshape(n, columns)
            out_ref[b, g * per : (g + 1) * per] = dot3(matrix, field).reshape(per, rows, columns)


def add_others(tiles, rate_ref, own_ref, received, out_ref, extra_ref=None):
    members, levels, rows, columns = own_ref.shape
    place = lax.axis_index("tile")
    rate = rate_ref[...]
    zero = jnp.zeros((levels, columns), F32)
    below, above = [zero] * members, [zero] * members
    for k in range(1, tiles):
        up = jnp.where(place >= k, jnp.exp(rate * (rows * (k - 1.0))), 0.0)
        down = jnp.where(place < k, jnp.exp(rate * (rows * (tiles - k - 1.0))), 0.0)
        for b in range(members):
            below[b] = below[b] + up * received[k - 1][b]
            above[b] = above[b] + down * received[k - 1][b]
    i = iota((rows, columns), 0)
    at = i.astype(F32)
    left = (2 * (rows * tiles - rows * place) - 2 * i).astype(F32)
    for l in range(levels):
        r = rate_ref[l : l + 1]
        from_below = jnp.exp(r * (at + 1.0)) * (1.0 - jnp.exp(r * left))
        from_above = jnp.exp(r * (rows - at))
        for b in range(members):
            total = own_ref[b, l] + (from_below * below[b][l : l + 1] + from_above * above[b][l : l + 1])
            out_ref[b, l] = total if extra_ref is None else total + extra_ref[b, l]


def indices(cells):
    whole = (cells + 0.5).astype(I32)
    return whole >> 7, whole & (LANES - 1)


def gather_kernel(tiles, blocks, rate_ref, own_ref, members_ref, *rest):
    received, rays = rest[: tiles - 1], rest[tiles - 1 : tiles - 1 + blocks]
    out_ref, smooth_ref, table_ref = rest[tiles - 1 + blocks :]
    add_others(tiles, rate_ref, own_ref, received, smooth_ref)
    members, levels, rows, columns = own_ref.shape
    high_rows = levels * rows
    for f in range(2):
        share = jnp.zeros((high_rows, columns), F32)
        for b in range(members):
            share = share + members_ref[b, f].reshape(high_rows, columns).astype(F32) * smooth_ref[b].reshape(
                high_rows, columns
            )
        high, low = split(share.T)
        table_ref[f * LANES : (f + 1) * LANES] = high
        table_ref[(f + 2) * LANES : (f + 3) * LANES] = low
    row_of = iota((high_rows, LANES), 0)
    lane_of = iota((LANES, LANES), 0)
    for block in range(blocks):
        ray = rays[block]

        def chunk(c, _, ray=ray, block=block):
            at = pl.ds(pl.multiple_of(c * 8, 8), 8)
            high, low = indices(ray[0, at, :])
            first, second = ray[1, at, :], ray[2, at, :]
            lines = []
            for pair in range(4):
                hot = jnp.concatenate(
                    [
                        jnp.where(row_of == high[r : r + 1], 1.0, 0.0).astype(BF16)
                        for r in (2 * pair, 2 * pair + 1)
                    ],
                    axis=1,
                )
                got = dot(table_ref[...], hot)
                for h in range(2):
                    r = 2 * pair + h
                    part = got[:, h * LANES : (h + 1) * LANES]
                    u = part[:LANES] + part[2 * LANES : 3 * LANES]
                    v = part[LANES : 2 * LANES] + part[3 * LANES :]
                    both = u * first[r : r + 1] + v * second[r : r + 1]
                    lines.append(
                        jnp.sum(jnp.where(lane_of == low[r : r + 1], both, 0.0), axis=0, keepdims=True)
                    )
            out_ref[block, at, :] = jnp.concatenate(lines, axis=0)
            return 0

        lax.fori_loop(0, ray.shape[1] // 8, chunk, 0)


def scatter_kernel(tiles, blocks, rate_ref, high_ref, low_ref, members_ref, own_ref, *rest):
    others, rays = rest[: blocks - 1], rest[blocks - 1 : 2 * blocks - 1]
    out_ref = rest[2 * blocks - 1]
    outs = rest[2 * blocks : 2 * blocks + tiles - 1]
    total_ref, mixed_ref = rest[2 * blocks + tiles - 1 :]
    members, levels, rows, columns = out_ref.shape
    high_rows = levels * rows
    row_of = iota((high_rows, LANES), 0)
    lane_of = iota((LANES, LANES), 0)
    total_ref[...] = jnp.zeros_like(total_ref)
    for block in range(blocks):
        ray = rays[block]

        def chunk(c, _, ray=ray, block=block):
            at = pl.ds(pl.multiple_of(c * 8, 8), 8)
            high, low = indices(ray[0, at, :])
            modelled = own_ref[block, at, :]
            for k in range(1, blocks):
                modelled = modelled + others[k - 1][block ^ k, at, :]
            departure = ray[4, at, :] * (modelled - ray[3, at, :])
            values = []
            for f in range(2):
                value = ray[1 + f, at, :] * departure
                part = value.astype(BF16).astype(F32)
                values.append((part, value - part))
            hots, sides = [], [[], []]
            for r in range(8):
                hots.append(jnp.where(row_of == high[r : r + 1], 1.0, 0.0).astype(BF16))
                here = lane_of == low[r : r + 1]
                for piece in range(2):
                    sides[piece].append(
                        jnp.concatenate(
                            [jnp.where(here, values[f][piece][r : r + 1], 0.0).astype(BF16) for f in range(2)],
                            axis=0,
                        )
                    )
            left = jnp.concatenate(hots, axis=1)
            dims = (((1,), (1,)), ((), ()))
            added = None
            for piece in range(2):
                right = jnp.concatenate(sides[piece], axis=1)
                term = lax.dot_general(left, right, dims, preferred_element_type=F32)
                added = term if added is None else added + term
            total_ref[...] += added
            return 0

        lax.fori_loop(0, ray.shape[1] // 8, chunk, 0)
    for l in range(levels):
        u = total_ref[l * rows : (l + 1) * rows, :LANES]
        v = total_ref[l * rows : (l + 1) * rows, LANES:]
        for b in range(members):
            mixed_ref[b, l] = members_ref[b, 0, l].astype(F32) * u + members_ref[b, 1, l].astype(F32) * v
    filter_levels(mixed_ref, mixed_ref)
    filter_columns(mixed_ref, high_ref, low_ref, out_ref)
    states(tiles, rate_ref, out_ref, outs)


def last_kernel(tiles, rate_ref, alpha_ref, own_ref, *rest):
    add_others(tiles, rate_ref, own_ref, rest[:-1], rest[-1], alpha_ref)


def call(body, outs, scratch=(), cost=None):
    def run(*args):
        return pl.pallas_call(
            body,
            out_shape=outs,
            in_specs=[VMEM] * len(args),
            out_specs=jax.tree.map(lambda _: VMEM, outs),
            scratch_shapes=list(scratch),
            compiler_params=PARAMS,
            cost_estimate=cost,
        )(*args)

    return run


def shaped(*shape, dtype=F32):
    return jax.ShapeDtypeStruct(shape, dtype)


def over_tiles(parts, tiles):
    return [
        lax.ppermute(part, "tile", [(i, (i + k) % tiles) for i in range(tiles)])
        for k, part in enumerate(parts, 1)
    ]


def over_members(part, blocks):
    return [lax.ppermute(part, "mem", [(i, i ^ k) for i in range(blocks)]) for k in range(1, blocks)]


def per_device(alpha, members, scales, observed, precision, ray_weights, cell_index, owner):
    tiles, blocks = lax.axis_size("tile"), lax.axis_size("mem")
    count_rays, gates = observed.shape
    capacity = 3 * count_rays // tiles
    per = -(-capacity * (gates // LANES) // blocks)
    shape = alpha.shape
    count, levels, rows, columns = shape
    sent = call(
        functools.partial(pack_rays_kernel, tiles, per),
        [shaped(FIELDS, per, LANES) for _ in range(tiles)],
    )(owner, cell_index, ray_weights, observed, precision)
    rate = jnp.broadcast_to((-1.0 / scales)[:, None], (levels, LANES))
    here = jnp.concatenate([sent[0], *over_tiles(sent[1:], tiles)], axis=1)
    rays = [here, *over_members(here, blocks)]

    state = shaped(count, levels, columns)
    high, low, field, *given = call(
        functools.partial(first_kernel, tiles),
        [shaped(levels, columns, columns, dtype=BF16)] * 2 + [shaped(*shape)] + [state] * (tiles - 1),
        [pltpu.VMEM(shape, F32)],
    )(rate, alpha)
    received = over_tiles(given, tiles)
    own = call(functools.partial(within_kernel, tiles), shaped(*shape))(rate, field)
    modelled = call(
        functools.partial(gather_kernel, tiles, blocks),
        shaped(blocks, tiles * per, LANES),
        [pltpu.VMEM(shape, F32), pltpu.VMEM((4 * LANES, levels * rows), BF16)],
    )(rate, own, members, *received, *rays)
    others = over_members(modelled, blocks)
    field, *given = call(
        functools.partial(scatter_kernel, tiles, blocks),
        [shaped(*shape)] + [state] * (tiles - 1),
        [pltpu.VMEM((levels * rows, 2 * LANES), F32), pltpu.VMEM(shape, F32)],
    )(rate, high, low, members, modelled, *others, *rays)
    received = over_tiles(given, tiles)
    own = call(functools.partial(within_kernel, tiles), shaped(*shape))(rate, field)
    return call(functools.partial(last_kernel, tiles), shaped(*shape))(rate, alpha, own, *received)


def solution(mesh):
    return jax.shard_map(
        per_device,
        mesh=mesh,
        in_specs=(
            P("mem", None, "tile", None),
            P("mem", None, None, "tile", None),
            P(),
            P("tile", None),
            P("tile", None),
            P("tile", None, None),
            P("tile", None),
            P("tile", None),
        ),
        out_specs=P("mem", None, "tile", None),
        check_vma=False,
    )
```

```python
import functools
import math

import jax
import jax.numpy as jnp
from jax import lax
from jax.experimental import pallas as pl
from jax.experimental.pallas import tpu as pltpu
from jax.sharding import PartitionSpec as P

F32 = jnp.float32
BF16 = jnp.bfloat16
I32 = jnp.int32
F8 = jnp.float8_e4m3fn
PIECES = 3
LANES = 128
Z_DECAY = math.exp(-1.0 / 3.0)
Z_GAIN = (1.0 - Z_DECAY) ** 2 * math.sqrt((1.0 + Z_DECAY) / (1.0 - Z_DECAY))
VMEM = pl.BlockSpec(memory_space=pltpu.VMEM)
COST = pl.CostEstimate(flops=2 * 10**10, bytes_accessed=4 * 10**6, transcendentals=0)
PARAMS = pltpu.CompilerParams(vmem_limit_bytes=48 * 1024 * 1024)


def split(x):
    high = x.astype(BF16)
    return high, (x - high.astype(F32)).astype(BF16)


def dot(a, b):
    return jnp.dot(a, b, preferred_element_type=F32)


def dot3(a, b):
    (ah, al), (bh, bl) = split(a), split(b)
    return dot(ah, bh) + (dot(ah, bl) + dot(al, bh))


def iota(shape, dim):
    return lax.broadcasted_iota(I32, shape, dim)


def norm_of(rate):
    x = -rate
    series = jnp.ones_like(x)
    for k in (8, 7, 6, 5, 4, 3, 2):
        series = 1.0 - series * x * (1.0 / k)
    return jnp.sqrt(x * series / (1.0 + jnp.exp(rate)))


def pack_rays_kernel(per, owner_ref, cell_ref, weights_ref, observed_ref, precision_ref, out_ref):
    rays, gates = observed_ref.shape
    halves = gates // LANES
    wide = out_ref.shape[0] * per
    owner = owner_ref[...]
    named = (owner == iota((rays, LANES), 1)).astype(F32)
    earlier = (iota((rays, rays), 0) > iota((rays, rays), 1)).astype(F32)
    rank = jnp.sum(dot(earlier, named) * named, axis=1, keepdims=True).astype(I32)
    column = iota((rays, -(-wide // LANES) * LANES), 1)
    target, row = column // per, column % per
    picks = [
        ((owner == target) & (rank * halves + half == row)).astype(F32).T[:wide] for half in range(halves)
    ]
    fields = (
        cell_ref[...].astype(F32),
        weights_ref[:, 0, :],
        weights_ref[:, 1, :],
        observed_ref[...],
        precision_ref[...],
    )
    for f, field in enumerate(fields):
        got = sum(
            jnp.dot(
                picks[half],
                field[:, half * LANES : (half + 1) * LANES],
                precision=lax.Precision.HIGHEST,
                preferred_element_type=F32,
            )
            for half in range(halves)
        )
        out_ref[:, f] = got.reshape(-1, per, LANES)


def filter_levels(field_ref, out_ref):
    levels = field_ref.shape[1]
    state = field_ref[:, 0]
    out_ref[:, 0] = state
    for l in range(1, levels):
        state = field_ref[:, l] + Z_DECAY * state
        out_ref[:, l] = state
    for l in range(levels - 2, -1, -1):
        state = out_ref[:, l] + Z_DECAY * state
        out_ref[:, l] = state


def filter_columns(field_ref, high_ref, low_ref, out_ref):
    members, levels, rows, columns = field_ref.shape

    def level(l, _):
        field = field_ref[:, l].reshape(members * rows, columns)
        high, low = split(field)
        both = dot(jnp.concatenate([high, low], axis=0), high_ref[l])
        total = both[: members * rows] + (both[members * rows :] + dot(high, low_ref[l]))
        out_ref[:, l] = total.reshape(members, rows, columns)
        return 0

    lax.fori_loop(0, levels, level, 0, unroll=4)


def columns_matrix(rate_ref, high_ref, low_ref):
    levels, n, _ = high_ref.shape
    i, j = iota((n, n), 0), iota((n, n), 1)
    dist = jnp.abs(i - j).astype(F32)
    left = (2 * (n - jnp.maximum(i, j))).astype(F32)

    def level(l, _):
        rate = rate_ref[pl.ds(l, 1), :]
        matrix = (Z_GAIN * norm_of(rate)) * jnp.exp(rate * dist) * (1.0 - jnp.exp(rate * left))
        high_ref[l], low_ref[l] = split(matrix)
        return 0

    lax.fori_loop(0, levels, level, 0, unroll=2)


def states(tiles, rate_ref, field_ref, outs):
    members, levels, rows, columns = field_ref.shape
    place = lax.axis_index("tile")
    per = LANES // rows
    level, column = iota((per, LANES), 0), iota((per, LANES), 1)
    same = level == column // rows
    at = (column % rows).astype(F32)
    left = (2 * (rows * tiles - rows * place) - 2 * (column % rows)).astype(F32)
    for g in range(levels // per):
        rate = rate_ref[g * per : (g + 1) * per]
        norm = norm_of(rate)
        forward = jnp.where(same, norm * jnp.exp(rate * (rows - 1.0 - at)), 0.0)
        backward = jnp.where(same, norm * jnp.exp(rate * at) * (1.0 - jnp.exp(rate * left)), 0.0)
        both = jnp.concatenate([forward, backward], axis=0)
        for b in range(members):
            field = field_ref[b, g * per : (g + 1) * per].reshape(per * rows, columns)
            got = dot3(both, field)
            for k in range(1, tiles):
                outs[k - 1][b, g * per : (g + 1) * per] = jnp.where(place + k < tiles, got[:per], got[per:])


def first_kernel(tiles, rate_ref, alpha_ref, high_ref, low_ref, out_ref, *rest):
    outs, scratch = rest[:-1], rest[-1]
    columns_matrix(rate_ref, high_ref, low_ref)
    filter_levels(alpha_ref, scratch)
    filter_columns(scratch, high_ref, low_ref, out_ref)
    states(tiles, rate_ref, out_ref, outs)


def within_kernel(tiles, rate_ref, field_ref, out_ref):
    members, levels, rows, columns = field_ref.shape
    place = lax.axis_index("tile")
    per = LANES // rows
    n = per * rows
    row, column = iota((n, n), 0), iota((n, n), 1)
    same = row // rows == column // rows
    i, j = row % rows, column % rows
    dist = jnp.abs(i - j).astype(F32)
    left = (2 * (rows * tiles - rows * place) - 2 * jnp.maximum(i, j)).astype(F32)
    for g in range(levels // per):
        rate = jnp.concatenate(
            [jnp.broadcast_to(rate_ref[l : l + 1], (rows, LANES)) for l in range(g * per, (g + 1) * per)], axis=0
        )
        matrix = jnp.where(same, norm_of(rate) * jnp.exp(rate * dist) * (1.0 - jnp.exp(rate * left)), 0.0)
        for b in range(members):
            field = field_ref[b, g * per : (g + 1) * per].reshape(n, columns)
            out_ref[b, g * per : (g + 1) * per] = dot3(matrix, field).reshape(per, rows, columns)


def add_others(tiles, rate_ref, own_ref, received, out_ref, extra_ref=None):
    members, levels, rows, columns = own_ref.shape
    place = lax.axis_index("tile")
    rate = rate_ref[...]
    zero = jnp.zeros((levels, columns), F32)
    below, above = [zero] * members, [zero] * members
    for k in range(1, tiles):
        up = jnp.where(place >= k, jnp.exp(rate * (rows * (k - 1.0))), 0.0)
        down = jnp.where(place < k, jnp.exp(rate * (rows * (tiles - k - 1.0))), 0.0)
        for b in range(members):
            below[b] = below[b] + up * received[k - 1][b]
            above[b] = above[b] + down * received[k - 1][b]
    i = iota((rows, columns), 0)
    at = i.astype(F32)
    left = (2 * (rows * tiles - rows * place) - 2 * i).astype(F32)
    for l in range(levels):
        r = rate_ref[l : l + 1]
        from_below = jnp.exp(r * (at + 1.0)) * (1.0 - jnp.exp(r * left))
        from_above = jnp.exp(r * (rows - at))
        for b in range(members):
            total = own_ref[b, l] + (from_below * below[b][l : l + 1] + from_above * above[b][l : l + 1])
            out_ref[b, l] = total if extra_ref is None else total + extra_ref[b, l]


def indices(cells):
    whole = (cells + 0.5).astype(I32)
    return whole >> 7, whole & (LANES - 1)


def chunks_of(shape):
    tiles, per = shape[0], shape[-2]

    def run(body):
        def step(c, _):
            body(c // (per // 8), pl.ds(pl.multiple_of(c % (per // 8) * 8, 8), 8))
            return 0

        lax.fori_loop(0, tiles * (per // 8), step, 0, unroll=8)

    return run


def hot_rows(high, row_of, high_rows):
    count, _ = row_of.shape
    one, zero = jnp.ones((), BF16), jnp.zeros((), BF16)
    high = high.astype(F32)
    blocks = high_rows // count

    def rows(r):
        line = high[r : r + 1]
        return jnp.concatenate(
            [jnp.where(row_of == (line - float(count * h)).astype(BF16), one, zero) for h in range(blocks)], axis=0
        )

    return rows


def gather_kernel(tiles, rate_ref, own_ref, members_ref, *rest):
    received, ray = rest[: tiles - 1], rest[tiles - 1]
    out_ref, smooth_ref, table_ref = rest[tiles:]
    add_others(tiles, rate_ref, own_ref, received, smooth_ref)
    members, levels, rows, columns = own_ref.shape
    high_rows = levels * rows
    shares = []
    for f in range(2):
        share = jnp.zeros((high_rows, columns), F32)
        for b in range(members):
            share = share + members_ref[b, f].reshape(high_rows, columns).astype(F32) * smooth_ref[b].reshape(
                high_rows, columns
            )
        shares.append(share)
    largest = jnp.maximum(jnp.max(jnp.maximum(jnp.abs(shares[0]), jnp.abs(shares[1]))), 1e-30)
    scale, back = 256.0 / largest, largest * (1.0 / 256.0)
    for f in range(2):
        rest_of = shares[f].T * scale
        for k in range(PIECES):
            piece = rest_of.astype(F8)
            table_ref[(2 * k + f) * LANES : (2 * k + f + 1) * LANES] = piece
            rest_of = (rest_of - piece.astype(F32)) * 16.0
    row_of = iota((256, LANES), 0).astype(F32).astype(BF16)
    lane_of = iota((LANES, LANES), 0)

    @chunks_of(out_ref.shape)
    def _(s, at):
        high, low = indices(ray[s, 0, at, :])
        hot_row = hot_rows(high, row_of, high_rows)
        first, second = ray[s, 1, at, :] * back, ray[s, 2, at, :] * back
        lines = []
        for pair in range(4):
            hot = jnp.concatenate([hot_row(2 * pair), hot_row(2 * pair + 1)], axis=1).astype(F8)
            got = dot(table_ref[...], hot)
            total = got[: 2 * LANES]
            for k in range(1, PIECES):
                total = total + got[2 * k * LANES : 2 * (k + 1) * LANES] * 16.0**-k
            for h in range(2):
                r = 2 * pair + h
                here = lane_of == low[r : r + 1]
                part = total[:, h * LANES : (h + 1) * LANES]
                u = jnp.sum(jnp.where(here, part[:LANES], 0.0), axis=0, keepdims=True)
                v = jnp.sum(jnp.where(here, part[LANES:], 0.0), axis=0, keepdims=True)
                lines.append(u * first[r : r + 1] + v * second[r : r + 1])
        out_ref[s, at, :] = jnp.concatenate(lines, axis=0)


def scatter_kernel(tiles, blocks, rate_ref, high_ref, low_ref, members_ref, ray, *rest):
    partial = rest[:blocks]
    out_ref = rest[blocks]
    outs = rest[blocks + 1 : blocks + tiles]
    total_ref, mixed_ref = rest[blocks + tiles :]
    members, levels, rows, columns = out_ref.shape
    high_rows = levels * rows
    row_of = iota((256, LANES), 0).astype(F32).astype(BF16)
    lane_of = iota((LANES, LANES), 0).astype(F32).astype(BF16)
    none = jnp.zeros((), BF16)
    total_ref[...] = jnp.zeros_like(total_ref)

    @chunks_of(partial[0].shape)
    def _(s, at):
        high, low = indices(ray[s, 0, at, :])
        hot_row = hot_rows(high, row_of, high_rows)
        low = low.astype(F32)
        modelled = partial[0][s, at, :]
        for other in partial[1:]:
            modelled = modelled + other[s, at, :]
        departure = ray[s, 4, at, :] * (modelled - ray[s, 3, at, :])
        values = []
        for f in range(2):
            value = ray[s, 1 + f, at, :] * departure
            part = value.astype(BF16).astype(F32)
            values.append((part, value - part))
        sides = [[], []]
        for r in range(8):
            here = lane_of == low[r : r + 1].astype(BF16)
            for piece in range(2):
                sides[piece].append(
                    jnp.concatenate(
                        [jnp.where(here, values[f][piece][r : r + 1].astype(BF16), none) for f in range(2)], axis=0
                    )
                )
        left = [hot_row(r) for r in range(8)]
        total_ref[...] += lax.dot_general(
            jnp.concatenate(left + left, axis=1),
            jnp.concatenate(sides[0] + sides[1], axis=1),
            (((1,), (1,)), ((), ())),
            preferred_element_type=F32,
        )

    for l in range(levels):
        u = total_ref[l * rows : (l + 1) * rows, :LANES]
        v = total_ref[l * rows : (l + 1) * rows, LANES:]
        for b in range(members):
            mixed_ref[b, l] = members_ref[b, 0, l].astype(F32) * u + members_ref[b, 1, l].astype(F32) * v
    filter_levels(mixed_ref, mixed_ref)
    filter_columns(mixed_ref, high_ref, low_ref, out_ref)
    states(tiles, rate_ref, out_ref, outs)


def last_kernel(tiles, rate_ref, alpha_ref, own_ref, *rest):
    add_others(tiles, rate_ref, own_ref, rest[:-1], rest[-1], alpha_ref)


def call(body, outs, scratch=(), cost=None):
    def run(*args):
        return pl.pallas_call(
            body,
            out_shape=outs,
            in_specs=[VMEM] * len(args),
            out_specs=jax.tree.map(lambda _: VMEM, outs),
            scratch_shapes=list(scratch),
            compiler_params=PARAMS,
            cost_estimate=cost,
        )(*args)

    return run


def shaped(*shape, dtype=F32):
    return jax.ShapeDtypeStruct(shape, dtype)


def over_tiles(parts, tiles):
    return [
        lax.ppermute(part, "tile", [(i, (i + k) % tiles) for i in range(tiles)])
        for k, part in enumerate(parts, 1)
    ]


def over_members(part, blocks):
    return [lax.ppermute(part, "mem", [(i, i ^ k) for i in range(blocks)]) for k in range(1, blocks)]


def per_device(alpha, members, scales, observed, precision, ray_weights, cell_index, owner):
    tiles, blocks = lax.axis_size("tile"), lax.axis_size("mem")
    count_rays, gates = observed.shape
    capacity = 3 * count_rays // tiles
    per = -(-capacity * (gates // LANES) // 8) * 8
    shape = alpha.shape
    count, levels, rows, columns = shape
    ray = call(functools.partial(pack_rays_kernel, per), shaped(tiles, 5, per, LANES))(
        owner, cell_index, ray_weights, observed, precision
    )
    ray = lax.all_to_all(ray, "tile", split_axis=0, concat_axis=0, tiled=True)
    rate = jnp.broadcast_to((-1.0 / scales)[:, None], (levels, LANES))

    state = shaped(count, levels, columns)
    high, low, field, *given = call(
        functools.partial(first_kernel, tiles),
        [shaped(levels, columns, columns, dtype=BF16)] * 2 + [shaped(*shape)] + [state] * (tiles - 1),
        [pltpu.VMEM(shape, F32)],
    )(rate, alpha)
    received = over_tiles(given, tiles)
    own = call(functools.partial(within_kernel, tiles), shaped(*shape))(rate, field)
    modelled = call(
        functools.partial(gather_kernel, tiles),
        shaped(tiles, per, LANES),
        [pltpu.VMEM(shape, F32), pltpu.VMEM((2 * PIECES * LANES, levels * rows), F8)],
        COST,
    )(rate, own, members, *received, ray)
    field, *given = call(
        functools.partial(scatter_kernel, tiles, blocks),
        [shaped(*shape)] + [state] * (tiles - 1),
        [pltpu.VMEM((levels * rows, 2 * LANES), F32), pltpu.VMEM(shape, F32)],
        COST,
    )(rate, high, low, members, ray, modelled, *over_members(modelled, blocks))
    received = over_tiles(given, tiles)
    own = call(functools.partial(within_kernel, tiles), shaped(*shape))(rate, field)
    return call(functools.partial(last_kernel, tiles), shaped(*shape))(rate, alpha, own, *received)


def solution(mesh):
    return jax.shard_map(
        per_device,
        mesh=mesh,
        in_specs=(
            P("mem", None, "tile", None),
            P("mem", None, None, "tile", None),
            P(),
            P("tile", None),
            P("tile", None),
            P("tile", None, None),
            P("tile", None),
            P("tile", None),
        ),
        out_specs=P("mem", None, "tile", None),
        check_vma=False,
    )
```

```python
import functools
import math

import jax
import jax.numpy as jnp
from jax import lax
from jax.experimental import pallas as pl
from jax.experimental.pallas import tpu as pltpu
from jax.sharding import PartitionSpec as P

F32 = jnp.float32
BF16 = jnp.bfloat16
I32 = jnp.int32
F8 = jnp.float8_e4m3fn
PIECES = 3
LANES = 128
Z_DECAY = math.exp(-1.0 / 3.0)
Z_GAIN = (1.0 - Z_DECAY) ** 2 * math.sqrt((1.0 + Z_DECAY) / (1.0 - Z_DECAY))
VMEM = pl.BlockSpec(memory_space=pltpu.VMEM)
COST = pl.CostEstimate(flops=2 * 10**10, bytes_accessed=4 * 10**6, transcendentals=0)
WIDE = pltpu.CompilerParams(vmem_limit_bytes=65000 * 1024)
PARAMS = pltpu.CompilerParams(vmem_limit_bytes=48 * 1024 * 1024)


def split(x):
    high = x.astype(BF16)
    return high, (x - high.astype(F32)).astype(BF16)


def dot(a, b):
    return jnp.dot(a, b, preferred_element_type=F32)


def dot3(a, b):
    (ah, al), (bh, bl) = split(a), split(b)
    return dot(ah, bh) + (dot(ah, bl) + dot(al, bh))


def iota(shape, dim):
    return lax.broadcasted_iota(I32, shape, dim)


def norm_of(rate):
    x = -rate
    series = jnp.ones_like(x)
    for k in (8, 7, 6, 5, 4, 3, 2):
        series = 1.0 - series * x * (1.0 / k)
    return jnp.sqrt(x * series / (1.0 + jnp.exp(rate)))


def pack_rays_kernel(per, *refs):
    given, (out_ref, rate_ref), held, sems = refs[:6], refs[6:8], refs[8:14], refs[14]
    copies = [pltpu.make_async_copy(given[k], held[k], sems.at[k]) for k in range(6)]
    for copy in copies:
        copy.start()
    for copy in copies:
        copy.wait()
    owner_ref, scales_ref, held = held[0], held[1], held[2:]
    levels = rate_ref.shape[0]
    here = iota((levels, levels), 0) == iota((levels, levels), 1)
    scale = jnp.sum(jnp.where(here, scales_ref[...], 0.0), axis=1, keepdims=True)
    rate_ref[...] = -1.0 / jnp.broadcast_to(scale, rate_ref.shape)
    rays, gates = held[0].shape
    tiles, halves = out_ref.shape[0], gates // LANES
    part = lax.axis_index("mem")
    row = iota((tiles * per, rays), 0)
    target, wanted = row // per, row % per + part * per
    named = owner_ref[...] == target
    earlier = (iota((rays, rays), 0) < iota((rays, rays), 1)).astype(F32)
    rank = dot(named.astype(F32), earlier).astype(I32)
    picks = jnp.concatenate(
        [(named & (rank * halves + half == wanted)).astype(F32) for half in range(halves)], axis=1
    )
    cell_ref, weights_ref, observed_ref, precision_ref = held
    fields = (
        cell_ref[...].astype(F32),
        weights_ref[:, 0, :],
        weights_ref[:, 1, :],
        observed_ref[...],
        precision_ref[...],
    )
    stacked = jnp.concatenate(
        [
            jnp.concatenate([field[:, h * LANES : (h + 1) * LANES] for h in range(halves)], axis=0)
            for field in fields
        ],
        axis=1,
    )
    got = jnp.dot(picks, stacked, precision=lax.Precision.HIGHEST, preferred_element_type=F32)
    for t in range(tiles):
        for f in range(len(fields)):
            out_ref[t, f * per : (f + 1) * per] = got[t * per : (t + 1) * per, f * LANES : (f + 1) * LANES]


def filter_levels(field_ref, out_ref):
    levels = field_ref.shape[1]
    state = field_ref[:, 0]
    out_ref[:, 0] = state
    for l in range(1, levels):
        state = field_ref[:, l] + Z_DECAY * state
        out_ref[:, l] = state
    for l in range(levels - 2, -1, -1):
        state = out_ref[:, l] + Z_DECAY * state
        out_ref[:, l] = state


def filter_columns(field_ref, high_ref, low_ref, out_ref):
    members, levels, rows, columns = field_ref.shape

    def level(l, _):
        field = field_ref[:, l].reshape(members * rows, columns)
        high, low = split(field)
        both = dot(jnp.concatenate([high, low], axis=0), high_ref[l])
        total = both[: members * rows] + (both[members * rows :] + dot(high, low_ref[l]))
        out_ref[:, l] = total.reshape(members, rows, columns)
        return 0

    lax.fori_loop(0, levels, level, 0, unroll=4)


def columns_matrix(rate_ref, high_ref, low_ref):
    levels, n, _ = high_ref.shape
    i, j = iota((n, n), 0), iota((n, n), 1)
    dist = jnp.abs(i - j).astype(F32)
    left = (2 * (n - jnp.maximum(i, j))).astype(F32)

    def level(l, _):
        rate = rate_ref[pl.ds(l, 1), :]
        matrix = (Z_GAIN * norm_of(rate)) * jnp.exp(rate * dist) * (1.0 - jnp.exp(rate * left))
        high_ref[l], low_ref[l] = split(matrix)
        return 0

    lax.fori_loop(0, levels, level, 0, unroll=2)


def states(tiles, rate_ref, field_ref, out_ref):
    members, levels, rows, columns = field_ref.shape
    place = lax.axis_index("tile")
    per = LANES // rows
    level, column = iota((per, LANES), 0), iota((per, LANES), 1)
    same = level == column // rows
    at = (column % rows).astype(F32)
    left = (2 * (rows * tiles - rows * place) - 2 * (column % rows)).astype(F32)
    for g in range(levels // per):
        rate = rate_ref[g * per : (g + 1) * per]
        norm = norm_of(rate)
        forward = jnp.where(same, norm * jnp.exp(rate * (rows - 1.0 - at)), 0.0)
        backward = jnp.where(same, norm * jnp.exp(rate * at) * (1.0 - jnp.exp(rate * left)), 0.0)
        both = jnp.concatenate([forward, backward], axis=0)
        for b in range(members):
            field = field_ref[b, g * per : (g + 1) * per].reshape(per * rows, columns)
            got = dot3(both, field)
            for way in range(2):
                out_ref[way, b, g * per : (g + 1) * per] = got[way * per : (way + 1) * per]


def chip_kernel(tiles, rows, rate_ref, own_ref, partner_ref, *outs):
    place = lax.axis_index("tile")
    chip, upper, chips = place // 2, place % 2 == 1, tiles // 2
    members = own_ref.shape[1]
    across = jnp.exp(rate_ref[...] * rows)
    for b in range(members):
        first = [jnp.where(upper, partner_ref[way, b], own_ref[way, b]) for way in range(2)]
        second = [jnp.where(upper, own_ref[way, b], partner_ref[way, b]) for way in range(2)]
        forward = across * first[0] + second[0]
        backward = first[1] + across * second[1]
        for k in range(1, chips):
            outs[k - 1][b] = jnp.where(chip + k < chips, forward, backward)


def first_kernel(tiles, rate_ref, alpha_ref, high_ref, low_ref, out_ref, state_ref, scratch):
    columns_matrix(rate_ref, high_ref, low_ref)
    filter_levels(alpha_ref, scratch)
    filter_columns(scratch, high_ref, low_ref, out_ref)
    states(tiles, rate_ref, out_ref, state_ref)


def within_kernel(tiles, rate_ref, field_ref, out_ref):
    members, levels, rows, columns = field_ref.shape
    place = lax.axis_index("tile")
    per = LANES // rows
    n = per * rows
    row, column = iota((n, n), 0), iota((n, n), 1)
    same = row // rows == column // rows
    i, j = row % rows, column % rows
    dist = jnp.abs(i - j).astype(F32)
    left = (2 * (rows * tiles - rows * place) - 2 * jnp.maximum(i, j)).astype(F32)
    for g in range(levels // per):
        rate = jnp.concatenate(
            [jnp.broadcast_to(rate_ref[l : l + 1], (rows, LANES)) for l in range(g * per, (g + 1) * per)], axis=0
        )
        matrix = jnp.where(same, norm_of(rate) * jnp.exp(rate * dist) * (1.0 - jnp.exp(rate * left)), 0.0)
        for b in range(members):
            field = field_ref[b, g * per : (g + 1) * per].reshape(n, columns)
            out_ref[b, g * per : (g + 1) * per] = dot3(matrix, field).reshape(per, rows, columns)


def add_others(tiles, rate_ref, own_ref, received, out_ref, extra_ref=None):
    members, levels, rows, columns = own_ref.shape
    partner_ref, received = received[0], received[1:]
    place = lax.axis_index("tile")
    chip, upper, chips = place // 2, place % 2, tiles // 2
    rate = rate_ref[...]
    below = [jnp.where(upper == 1, partner_ref[0, b], 0.0) for b in range(members)]
    above = [jnp.where(upper == 0, partner_ref[1, b], 0.0) for b in range(members)]
    for k in range(1, chips):
        up = jnp.where(chip >= k, jnp.exp(rate * (rows * (2 * (k - 1) + upper)).astype(F32)), 0.0)
        down = jnp.where(chip < k, jnp.exp(rate * (rows * (2 * (chips - k) - 1 - upper)).astype(F32)), 0.0)
        for b in range(members):
            below[b] = below[b] + up * received[k - 1][b]
            above[b] = above[b] + down * received[k - 1][b]
    i = iota((rows, columns), 0)
    at = i.astype(F32)
    left = (2 * (rows * tiles - rows * place) - 2 * i).astype(F32)
    for l in range(levels):
        r = rate_ref[l : l + 1]
        from_below = jnp.exp(r * (at + 1.0)) * (1.0 - jnp.exp(r * left))
        from_above = jnp.exp(r * (rows - at))
        for b in range(members):
            total = own_ref[b, l] + (from_below * below[b][l : l + 1] + from_above * above[b][l : l + 1])
            out_ref[b, l] = total if extra_ref is None else total + extra_ref[b, l]


def indices(cells):
    whole = (cells + 0.5).astype(I32)
    return whole >> 7, whole & (LANES - 1)


def chunks_of(count):
    def run(body):
        def step(c, _):
            body(pl.ds(pl.multiple_of(c * 8, 8), 8))
            return 0

        lax.fori_loop(0, count // 8, step, 0, unroll=8)

    return run


def hot_rows(high, row_of, high_rows):
    count, _ = row_of.shape
    one, zero = jnp.ones((), BF16), jnp.zeros((), BF16)
    high = high.astype(F32)
    blocks = high_rows // count

    def rows(r):
        line = high[r : r + 1]
        return jnp.concatenate(
            [jnp.where(row_of == (line - float(count * h)).astype(BF16), one, zero) for h in range(blocks)], axis=0
        )

    return rows


def gather_kernel(tiles, blocks, per, rate_ref, own_ref, members_ref, *rest):
    received, rays = rest[: tiles // 2], rest[tiles // 2 : tiles // 2 + blocks]
    out_ref, ray_ref, smooth_ref, table_ref = rest[tiles // 2 + blocks :]
    for p in range(blocks):
        for s in range(tiles):
            to = (p * tiles + s) * per
            for f in range(5):
                ray_ref[f, to : to + per] = rays[p][s, f * per : (f + 1) * per]
    add_others(tiles, rate_ref, own_ref, received, smooth_ref)
    members, levels, rows, columns = own_ref.shape
    high_rows = levels * rows
    shares = []
    for f in range(2):
        share = jnp.zeros((high_rows, columns), F32)
        for b in range(members):
            share = share + members_ref[b, f].reshape(high_rows, columns).astype(F32) * smooth_ref[b].reshape(
                high_rows, columns
            )
        shares.append(share)
    largest = jnp.maximum(jnp.max(jnp.maximum(jnp.abs(shares[0]), jnp.abs(shares[1]))), 1e-30)
    scale, back = 256.0 / largest, largest * (1.0 / 256.0)
    for f in range(2):
        rest_of = shares[f].T * scale
        for k in range(PIECES):
            piece = rest_of.astype(F8)
            table_ref[(2 * k + f) * LANES : (2 * k + f + 1) * LANES] = piece
            rest_of = (rest_of - piece.astype(F32)) * 16.0
    row_of = iota((256, LANES), 0).astype(F32).astype(BF16)
    lane_of = iota((LANES, LANES), 0)

    @chunks_of(out_ref.shape[0])
    def _(at):
        high, low = indices(ray_ref[0, at, :])
        hot_row = hot_rows(high, row_of, high_rows)
        first, second = ray_ref[1, at, :] * back, ray_ref[2, at, :] * back
        lines = []
        for pair in range(4):
            hot = jnp.concatenate([hot_row(2 * pair), hot_row(2 * pair + 1)], axis=1).astype(F8)
            got = dot(table_ref[...], hot)
            total = got[: 2 * LANES]
            for k in range(1, PIECES):
                total = total + got[2 * k * LANES : 2 * (k + 1) * LANES] * 16.0**-k
            for h in range(2):
                r = 2 * pair + h
                here = lane_of == low[r : r + 1]
                part = total[:, h * LANES : (h + 1) * LANES]
                u = jnp.sum(jnp.where(here, part[:LANES], 0.0), axis=0, keepdims=True)
                v = jnp.sum(jnp.where(here, part[LANES:], 0.0), axis=0, keepdims=True)
                lines.append(u * first[r : r + 1] + v * second[r : r + 1])
        out_ref[at, :] = jnp.concatenate(lines, axis=0)


def scatter_kernel(tiles, blocks, rate_ref, high_ref, low_ref, members_ref, ray_ref, *rest):
    partial, (out_ref, state_ref, total_ref, mixed_ref, value_ref) = rest[:blocks], rest[blocks:]
    size = ray_ref.shape[1] // blocks
    for p in range(blocks):
        mine = slice(p * size, (p + 1) * size)
        modelled = partial[0][mine]
        for k in range(1, blocks):
            modelled = modelled + partial[k][(p ^ k) * size : ((p ^ k) + 1) * size]
        departure = ray_ref[4, mine] * (modelled - ray_ref[3, mine])
        for f in range(2):
            value_ref[f, mine] = ray_ref[1 + f, mine] * departure
    members, levels, rows, columns = out_ref.shape
    high_rows = levels * rows
    row_of = iota((256, LANES), 0).astype(F32).astype(BF16)
    lane_of = iota((LANES, LANES), 0).astype(F32).astype(BF16)
    none = jnp.zeros((), BF16)
    total_ref[...] = jnp.zeros_like(total_ref)

    @chunks_of(ray_ref.shape[1])
    def _(at):
        high, low = indices(ray_ref[0, at, :])
        hot_row = hot_rows(high, row_of, high_rows)
        low = low.astype(F32)
        values = []
        for f in range(2):
            value = value_ref[f, at, :]
            part = value.astype(BF16).astype(F32)
            values.append((part, value - part))
        sides = [[], []]
        for r in range(8):
            here = lane_of == low[r : r + 1].astype(BF16)
            for piece in range(2):
                sides[piece].append(
                    jnp.concatenate(
                        [jnp.where(here, values[f][piece][r : r + 1].astype(BF16), none) for f in range(2)], axis=0
                    )
                )
        left = [hot_row(r) for r in range(8)]
        total_ref[...] += lax.dot_general(
            jnp.concatenate(left + left, axis=1),
            jnp.concatenate(sides[0] + sides[1], axis=1),
            (((1,), (1,)), ((), ())),
            preferred_element_type=F32,
        )

    for l in range(levels):
        u = total_ref[l * rows : (l + 1) * rows, :LANES]
        v = total_ref[l * rows : (l + 1) * rows, LANES:]
        for b in range(members):
            mixed_ref[b, l] = members_ref[b, 0, l].astype(F32) * u + members_ref[b, 1, l].astype(F32) * v
    filter_levels(mixed_ref, mixed_ref)
    filter_columns(mixed_ref, high_ref, low_ref, out_ref)
    states(tiles, rate_ref, out_ref, state_ref)


def last_kernel(tiles, rate_ref, alpha_ref, own_ref, *rest):
    add_others(tiles, rate_ref, own_ref, rest[:-1], rest[-1], alpha_ref)


def call(body, outs, scratch=(), cost=None, specs=None, params=PARAMS):
    def run(*args):
        return pl.pallas_call(
            body,
            out_shape=outs,
            in_specs=specs or [VMEM] * len(args),
            out_specs=jax.tree.map(lambda _: VMEM, outs),
            scratch_shapes=list(scratch),
            compiler_params=params,
            cost_estimate=cost,
        )(*args)

    return run


def shaped(*shape, dtype=F32):
    return jax.ShapeDtypeStruct(shape, dtype)


def over_members(part, blocks):
    return [lax.ppermute(part, "mem", [(i, i ^ k) for i in range(blocks)]) for k in range(1, blocks)]


def exchange(rate, own, rows, tiles):
    chips = tiles // 2
    partner = lax.ppermute(own, "tile", [(i, i ^ 1) for i in range(tiles)])
    given = call(functools.partial(chip_kernel, tiles, rows), [shaped(*own.shape[1:])] * (chips - 1))(
        rate, own, partner
    )
    return [
        partner,
        *(
            lax.ppermute(
                part, "tile", [(2 * c + h, 2 * ((c + k) % chips) + h) for c in range(chips) for h in range(2)]
            )
            for k, part in enumerate(given, 1)
        ),
    ]


def per_device(alpha, members, scales, observed, precision, ray_weights, cell_index, owner):
    tiles, blocks = lax.axis_size("tile"), lax.axis_size("mem")
    count_rays, gates = observed.shape
    capacity = 3 * count_rays // tiles
    per = -(-capacity * (gates // LANES) // blocks)
    shape = alpha.shape
    count, levels, rows, columns = shape
    anywhere = pl.BlockSpec(memory_space=pltpu.HBM)
    given = (
        owner.reshape(1, count_rays),
        scales.reshape(1, levels),
        cell_index,
        ray_weights,
        observed,
        precision,
    )
    sent, rate = call(
        functools.partial(pack_rays_kernel, per),
        [shaped(tiles, 5 * per, LANES), shaped(levels, LANES)],
        [*(pltpu.VMEM(x.shape, x.dtype) for x in given), pltpu.SemaphoreType.DMA((6,))],
        specs=[anywhere] * 6,
        params=WIDE,
    )(*given)
    here = lax.all_to_all(sent, "tile", split_axis=0, concat_axis=0, tiled=True)
    rays = [here, *over_members(here, blocks)]

    state = shaped(2, count, levels, columns)
    high, low, field, own = call(
        functools.partial(first_kernel, tiles),
        [shaped(levels, columns, columns, dtype=BF16)] * 2 + [shaped(*shape), state],
        [pltpu.VMEM(shape, F32)],
    )(rate, alpha)
    received = exchange(rate, own, rows, tiles)
    own = call(functools.partial(within_kernel, tiles), shaped(*shape))(rate, field)
    total = blocks * tiles * per
    modelled, ray = call(
        functools.partial(gather_kernel, tiles, blocks, per),
        [shaped(total, LANES), shaped(5, total, LANES)],
        [pltpu.VMEM(shape, F32), pltpu.VMEM((2 * PIECES * LANES, levels * rows), F8)],
        COST,
    )(rate, own, members, *received, *rays)
    field, own = call(
        functools.partial(scatter_kernel, tiles, blocks),
        [shaped(*shape), state],
        [
            pltpu.VMEM((levels * rows, 2 * LANES), F32),
            pltpu.VMEM(shape, F32),
            pltpu.VMEM((2, total, LANES), F32),
        ],
        COST,
    )(rate, high, low, members, ray, modelled, *over_members(modelled, blocks))
    received = exchange(rate, own, rows, tiles)
    own = call(functools.partial(within_kernel, tiles), shaped(*shape))(rate, field)
    return call(functools.partial(last_kernel, tiles), shaped(*shape))(rate, alpha, own, *received)


def solution(mesh):
    return jax.shard_map(
        per_device,
        mesh=mesh,
        in_specs=(
            P("mem", None, "tile", None),
            P("mem", None, None, "tile", None),
            P(),
            P("tile", None),
            P("tile", None),
            P("tile", None, None),
            P("tile", None),
            P("tile", None),
        ),
        out_specs=P("mem", None, "tile", None),
        check_vma=False,
    )
```

```python
import functools
import math

import jax
import jax.numpy as jnp
from jax import lax
from jax.experimental import pallas as pl
from jax.experimental.pallas import tpu as pltpu
from jax.sharding import PartitionSpec as P

F32 = jnp.float32
BF16 = jnp.bfloat16
I32 = jnp.int32
F8 = jnp.float8_e4m3fn
PIECES = 3
LANES = 128
Z_DECAY = math.exp(-1.0 / 3.0)
Z_GAIN = (1.0 - Z_DECAY) ** 2 * math.sqrt((1.0 + Z_DECAY) / (1.0 - Z_DECAY))
VMEM = pl.BlockSpec(memory_space=pltpu.VMEM)
COST = pl.CostEstimate(flops=2 * 10**10, bytes_accessed=4 * 10**6, transcendentals=0)
WIDE = pltpu.CompilerParams(vmem_limit_bytes=65000 * 1024)
PARAMS = pltpu.CompilerParams(vmem_limit_bytes=48 * 1024 * 1024)


def split(x):
    high = x.astype(BF16)
    return high, (x - high.astype(F32)).astype(BF16)


def dot(a, b):
    return jnp.dot(a, b, preferred_element_type=F32)


def dot3(a, b):
    (ah, al), (bh, bl) = split(a), split(b)
    return dot(ah, bh) + (dot(ah, bl) + dot(al, bh))


def iota(shape, dim):
    return lax.broadcasted_iota(I32, shape, dim)


def norm_of(rate):
    x = -rate
    series = jnp.ones_like(x)
    for k in (8, 7, 6, 5, 4, 3, 2):
        series = 1.0 - series * x * (1.0 / k)
    return jnp.sqrt(x * series / (1.0 + jnp.exp(rate)))


def pack_rays_kernel(per, *refs):
    given, (out_ref, rate_ref), held, sems = refs[:6], refs[6:8], refs[8:14], refs[14]
    copies = [pltpu.make_async_copy(given[k], held[k], sems.at[k]) for k in range(6)]
    for copy in copies:
        copy.start()
    for copy in copies:
        copy.wait()
    owner_ref, scales_ref, held = held[0], held[1], held[2:]
    levels = rate_ref.shape[0]
    here = iota((levels, levels), 0) == iota((levels, levels), 1)
    scale = jnp.sum(jnp.where(here, scales_ref[...], 0.0), axis=1, keepdims=True)
    rate_ref[...] = -1.0 / jnp.broadcast_to(scale, rate_ref.shape)
    rays, gates = held[0].shape
    tiles, halves = out_ref.shape[0], gates // LANES
    row = iota((tiles * per, rays), 0)
    target, wanted = row // per, row % per
    named = owner_ref[...] == target
    earlier = (iota((rays, rays), 0) < iota((rays, rays), 1)).astype(F32)
    rank = dot(named.astype(F32), earlier).astype(I32)
    picks = jnp.concatenate(
        [(named & (rank * halves + half == wanted)).astype(F32) for half in range(halves)], axis=1
    )
    cell_ref, weights_ref, observed_ref, precision_ref = held
    fields = (
        cell_ref[...].astype(F32),
        weights_ref[:, 0, :],
        weights_ref[:, 1, :],
        observed_ref[...],
        precision_ref[...],
    )
    stacked = jnp.concatenate(
        [
            jnp.concatenate([field[:, h * LANES : (h + 1) * LANES] for h in range(halves)], axis=0)
            for field in fields
        ],
        axis=1,
    )
    got = jnp.dot(picks, stacked, precision=lax.Precision.HIGHEST, preferred_element_type=F32)
    for t in range(tiles):
        for f in range(len(fields)):
            out_ref[t, f * per : (f + 1) * per] = got[t * per : (t + 1) * per, f * LANES : (f + 1) * LANES]


def filter_levels(field_ref, out_ref):
    levels = field_ref.shape[1]
    state = field_ref[:, 0]
    out_ref[:, 0] = state
    for l in range(1, levels):
        state = field_ref[:, l] + Z_DECAY * state
        out_ref[:, l] = state
    for l in range(levels - 2, -1, -1):
        state = out_ref[:, l] + Z_DECAY * state
        out_ref[:, l] = state


def filter_columns(field_ref, high_ref, low_ref, out_ref):
    members, levels, rows, columns = field_ref.shape

    def level(l, _):
        field = field_ref[:, l].reshape(members * rows, columns)
        high, low = split(field)
        both = dot(jnp.concatenate([high, low], axis=0), high_ref[l])
        total = both[: members * rows] + (both[members * rows :] + dot(high, low_ref[l]))
        out_ref[:, l] = total.reshape(members, rows, columns)
        return 0

    lax.fori_loop(0, levels, level, 0, unroll=4)


def columns_matrix(rate_ref, high_ref, low_ref):
    levels, n, _ = high_ref.shape
    i, j = iota((n, n), 0), iota((n, n), 1)
    dist = jnp.abs(i - j).astype(F32)
    left = (2 * (n - jnp.maximum(i, j))).astype(F32)

    def level(l, _):
        rate = rate_ref[pl.ds(l, 1), :]
        matrix = (Z_GAIN * norm_of(rate)) * jnp.exp(rate * dist) * (1.0 - jnp.exp(rate * left))
        high_ref[l], low_ref[l] = split(matrix)
        return 0

    lax.fori_loop(0, levels, level, 0, unroll=2)


def states(tiles, rate_ref, field_ref, out_ref):
    members, levels, rows, columns = field_ref.shape
    place = lax.axis_index("tile")
    per = LANES // rows
    level, column = iota((per, LANES), 0), iota((per, LANES), 1)
    same = level == column // rows
    at = (column % rows).astype(F32)
    left = (2 * (rows * tiles - rows * place) - 2 * (column % rows)).astype(F32)
    for g in range(levels // per):
        rate = rate_ref[g * per : (g + 1) * per]
        norm = norm_of(rate)
        forward = jnp.where(same, norm * jnp.exp(rate * (rows - 1.0 - at)), 0.0)
        backward = jnp.where(same, norm * jnp.exp(rate * at) * (1.0 - jnp.exp(rate * left)), 0.0)
        both = jnp.concatenate([forward, backward], axis=0)
        for b in range(members):
            field = field_ref[b, g * per : (g + 1) * per].reshape(per * rows, columns)
            got = dot3(both, field)
            for way in range(2):
                out_ref[way, b, g * per : (g + 1) * per] = got[way * per : (way + 1) * per]


def chip_kernel(tiles, rows, rate_ref, own_ref, partner_ref, *outs):
    place = lax.axis_index("tile")
    chip, upper, chips = place // 2, place % 2 == 1, tiles // 2
    members = own_ref.shape[1]
    across = jnp.exp(rate_ref[...] * rows)
    for b in range(members):
        first = [jnp.where(upper, partner_ref[way, b], own_ref[way, b]) for way in range(2)]
        second = [jnp.where(upper, own_ref[way, b], partner_ref[way, b]) for way in range(2)]
        forward = across * first[0] + second[0]
        backward = first[1] + across * second[1]
        for k in range(1, chips):
            outs[k - 1][b] = jnp.where(chip + k < chips, forward, backward)


def first_kernel(tiles, rate_ref, alpha_ref, high_ref, low_ref, out_ref, state_ref, scratch):
    columns_matrix(rate_ref, high_ref, low_ref)
    filter_levels(alpha_ref, scratch)
    filter_columns(scratch, high_ref, low_ref, out_ref)
    states(tiles, rate_ref, out_ref, state_ref)


def within_kernel(tiles, rate_ref, field_ref, out_ref):
    members, levels, rows, columns = field_ref.shape
    place = lax.axis_index("tile")
    per = LANES // rows
    n = per * rows
    row, column = iota((n, n), 0), iota((n, n), 1)
    same = row // rows == column // rows
    i, j = row % rows, column % rows
    dist = jnp.abs(i - j).astype(F32)
    left = (2 * (rows * tiles - rows * place) - 2 * jnp.maximum(i, j)).astype(F32)
    for g in range(levels // per):
        rate = jnp.concatenate(
            [jnp.broadcast_to(rate_ref[l : l + 1], (rows, LANES)) for l in range(g * per, (g + 1) * per)], axis=0
        )
        matrix = jnp.where(same, norm_of(rate) * jnp.exp(rate * dist) * (1.0 - jnp.exp(rate * left)), 0.0)
        for b in range(members):
            field = field_ref[b, g * per : (g + 1) * per].reshape(n, columns)
            out_ref[b, g * per : (g + 1) * per] = dot3(matrix, field).reshape(per, rows, columns)


def add_others(tiles, rate_ref, own_ref, received, out_ref, extra_ref=None):
    members, levels, rows, columns = own_ref.shape
    partner_ref, received = received[0], received[1:]
    place = lax.axis_index("tile")
    chip, upper, chips = place // 2, place % 2, tiles // 2
    rate = rate_ref[...]
    below = [jnp.where(upper == 1, partner_ref[0, b], 0.0) for b in range(members)]
    above = [jnp.where(upper == 0, partner_ref[1, b], 0.0) for b in range(members)]
    for k in range(1, chips):
        up = jnp.where(chip >= k, jnp.exp(rate * (rows * (2 * (k - 1) + upper)).astype(F32)), 0.0)
        down = jnp.where(chip < k, jnp.exp(rate * (rows * (2 * (chips - k) - 1 - upper)).astype(F32)), 0.0)
        for b in range(members):
            below[b] = below[b] + up * received[k - 1][b]
            above[b] = above[b] + down * received[k - 1][b]
    i = iota((rows, columns), 0)
    at = i.astype(F32)
    left = (2 * (rows * tiles - rows * place) - 2 * i).astype(F32)
    for l in range(levels):
        r = rate_ref[l : l + 1]
        from_below = jnp.exp(r * (at + 1.0)) * (1.0 - jnp.exp(r * left))
        from_above = jnp.exp(r * (rows - at))
        for b in range(members):
            total = own_ref[b, l] + (from_below * below[b][l : l + 1] + from_above * above[b][l : l + 1])
            out_ref[b, l] = total if extra_ref is None else total + extra_ref[b, l]


def indices(cells):
    whole = (cells + 0.5).astype(I32)
    return whole >> 7, whole & (LANES - 1)


def chunks_of(count):
    def run(body):
        def step(c, _):
            body(pl.ds(pl.multiple_of(c * 8, 8), 8))
            return 0

        lax.fori_loop(0, count // 8, step, 0, unroll=8)

    return run


def hot_rows(high, row_of, high_rows):
    count, _ = row_of.shape
    one, zero = jnp.ones((), BF16), jnp.zeros((), BF16)
    high = high.astype(F32)
    blocks = high_rows // count

    def rows(r):
        line = high[r : r + 1]
        return jnp.concatenate(
            [jnp.where(row_of == (line - float(count * h)).astype(BF16), one, zero) for h in range(blocks)], axis=0
        )

    return rows


def gather_kernel(tiles, per, rate_ref, own_ref, members_ref, *rest):
    received, rays = rest[: tiles // 2], rest[tiles // 2]
    out_ref, ray_ref, smooth_ref, table_ref = rest[tiles // 2 + 1 :]
    for s in range(tiles):
        for f in range(5):
            ray_ref[f, s * per : (s + 1) * per] = rays[s, f * per : (f + 1) * per]
    add_others(tiles, rate_ref, own_ref, received, smooth_ref)
    members, levels, rows, columns = own_ref.shape
    high_rows = levels * rows
    shares = []
    for f in range(2):
        share = jnp.zeros((high_rows, columns), F32)
        for b in range(members):
            share = share + members_ref[b, f].reshape(high_rows, columns).astype(F32) * smooth_ref[b].reshape(
                high_rows, columns
            )
        shares.append(share)
    largest = jnp.maximum(jnp.max(jnp.maximum(jnp.abs(shares[0]), jnp.abs(shares[1]))), 1e-30)
    scale, back = 256.0 / largest, largest * (1.0 / 256.0)
    for f in range(2):
        rest_of = shares[f].T * scale
        for k in range(PIECES):
            piece = rest_of.astype(F8)
            table_ref[(2 * k + f) * LANES : (2 * k + f + 1) * LANES] = piece
            rest_of = (rest_of - piece.astype(F32)) * 16.0
    row_of = iota((256, LANES), 0).astype(F32).astype(BF16)
    lane_of = iota((LANES, LANES), 0)

    @chunks_of(out_ref.shape[0])
    def _(at):
        high, low = indices(ray_ref[0, at, :])
        hot_row = hot_rows(high, row_of, high_rows)
        first, second = ray_ref[1, at, :] * back, ray_ref[2, at, :] * back
        lines = []
        for pair in range(4):
            hot = jnp.concatenate([hot_row(2 * pair), hot_row(2 * pair + 1)], axis=1).astype(F8)
            got = dot(table_ref[...], hot)
            total = got[: 2 * LANES]
            for k in range(1, PIECES):
                total = total + got[2 * k * LANES : 2 * (k + 1) * LANES] * 16.0**-k
            for h in range(2):
                r = 2 * pair + h
                here = lane_of == low[r : r + 1]
                part = total[:, h * LANES : (h + 1) * LANES]
                u = jnp.sum(jnp.where(here, part[:LANES], 0.0), axis=0, keepdims=True)
                v = jnp.sum(jnp.where(here, part[LANES:], 0.0), axis=0, keepdims=True)
                lines.append(u * first[r : r + 1] + v * second[r : r + 1])
        out_ref[at, :] = jnp.concatenate(lines, axis=0)


def scatter_kernel(tiles, blocks, rate_ref, high_ref, low_ref, members_ref, ray_ref, *rest):
    partial, (out_ref, state_ref, total_ref, mixed_ref, value_ref) = rest[:blocks], rest[blocks:]
    modelled = partial[0][...]
    for other in partial[1:]:
        modelled = modelled + other[...]
    departure = ray_ref[4] * (modelled - ray_ref[3])
    for f in range(2):
        value_ref[f] = ray_ref[1 + f] * departure
    members, levels, rows, columns = out_ref.shape
    high_rows = levels * rows
    row_of = iota((256, LANES), 0).astype(F32).astype(BF16)
    lane_of = iota((LANES, LANES), 0).astype(F32).astype(BF16)
    none = jnp.zeros((), BF16)
    total_ref[...] = jnp.zeros_like(total_ref)

    @chunks_of(ray_ref.shape[1])
    def _(at):
        high, low = indices(ray_ref[0, at, :])
        hot_row = hot_rows(high, row_of, high_rows)
        low = low.astype(F32)
        values = []
        for f in range(2):
            value = value_ref[f, at, :]
            part = value.astype(BF16).astype(F32)
            values.append((part, value - part))
        sides = [[], []]
        for r in range(8):
            here = lane_of == low[r : r + 1].astype(BF16)
            for piece in range(2):
                sides[piece].append(
                    jnp.concatenate(
                        [jnp.where(here, values[f][piece][r : r + 1].astype(BF16), none) for f in range(2)], axis=0
                    )
                )
        left = [hot_row(r) for r in range(8)]
        total_ref[...] += lax.dot_general(
            jnp.concatenate(left + left, axis=1),
            jnp.concatenate(sides[0] + sides[1], axis=1),
            (((1,), (1,)), ((), ())),
            preferred_element_type=F32,
        )

    for l in range(levels):
        u = total_ref[l * rows : (l + 1) * rows, :LANES]
        v = total_ref[l * rows : (l + 1) * rows, LANES:]
        for b in range(members):
            mixed_ref[b, l] = members_ref[b, 0, l].astype(F32) * u + members_ref[b, 1, l].astype(F32) * v
    filter_levels(mixed_ref, mixed_ref)
    filter_columns(mixed_ref, high_ref, low_ref, out_ref)
    states(tiles, rate_ref, out_ref, state_ref)


def last_kernel(tiles, rate_ref, alpha_ref, own_ref, *rest):
    add_others(tiles, rate_ref, own_ref, rest[:-1], rest[-1], alpha_ref)


def call(body, outs, scratch=(), cost=None, specs=None, params=PARAMS):
    def run(*args):
        return pl.pallas_call(
            body,
            out_shape=outs,
            in_specs=specs or [VMEM] * len(args),
            out_specs=jax.tree.map(lambda _: VMEM, outs),
            scratch_shapes=list(scratch),
            compiler_params=params,
            cost_estimate=cost,
        )(*args)

    return run


def shaped(*shape, dtype=F32):
    return jax.ShapeDtypeStruct(shape, dtype)


def over_members(part, blocks):
    return [lax.ppermute(part, "mem", [(i, i ^ k) for i in range(blocks)]) for k in range(1, blocks)]


def exchange(rate, own, rows, tiles):
    chips = tiles // 2
    partner = lax.ppermute(own, "tile", [(i, i ^ 1) for i in range(tiles)])
    given = call(functools.partial(chip_kernel, tiles, rows), [shaped(*own.shape[1:])] * (chips - 1))(
        rate, own, partner
    )
    return [
        partner,
        *(
            lax.ppermute(
                part, "tile", [(2 * c + h, 2 * ((c + k) % chips) + h) for c in range(chips) for h in range(2)]
            )
            for k, part in enumerate(given, 1)
        ),
    ]


def per_device(alpha, members, scales, observed, precision, ray_weights, cell_index, owner):
    tiles, blocks = lax.axis_size("tile"), lax.axis_size("mem")
    count_rays, gates = observed.shape
    capacity = 3 * count_rays // tiles
    per = capacity * (gates // LANES)
    shape = alpha.shape
    count, levels, rows, columns = shape
    anywhere = pl.BlockSpec(memory_space=pltpu.HBM)
    given = (
        owner.reshape(1, count_rays),
        scales.reshape(1, levels),
        cell_index,
        ray_weights,
        observed,
        precision,
    )
    sent, rate = call(
        functools.partial(pack_rays_kernel, per),
        [shaped(tiles, 5 * per, LANES), shaped(levels, LANES)],
        [*(pltpu.VMEM(x.shape, x.dtype) for x in given), pltpu.SemaphoreType.DMA((6,))],
        specs=[anywhere] * 6,
        params=WIDE,
    )(*given)
    here = lax.all_to_all(sent, "tile", split_axis=0, concat_axis=0, tiled=True)

    state = shaped(2, count, levels, columns)
    high, low, field, own = call(
        functools.partial(first_kernel, tiles),
        [shaped(levels, columns, columns, dtype=BF16)] * 2 + [shaped(*shape), state],
        [pltpu.VMEM(shape, F32)],
    )(rate, alpha)
    received = exchange(rate, own, rows, tiles)
    own = call(functools.partial(within_kernel, tiles), shaped(*shape))(rate, field)
    total = tiles * per
    modelled, ray = call(
        functools.partial(gather_kernel, tiles, per),
        [shaped(total, LANES), shaped(5, total, LANES)],
        [pltpu.VMEM(shape, F32), pltpu.VMEM((2 * PIECES * LANES, levels * rows), F8)],
        COST,
    )(rate, own, members, *received, here)
    field, own = call(
        functools.partial(scatter_kernel, tiles, blocks),
        [shaped(*shape), state],
        [
            pltpu.VMEM((levels * rows, 2 * LANES), F32),
            pltpu.VMEM(shape, F32),
            pltpu.VMEM((2, total, LANES), F32),
        ],
        COST,
    )(rate, high, low, members, ray, modelled, *over_members(modelled, blocks))
    received = exchange(rate, own, rows, tiles)
    own = call(functools.partial(within_kernel, tiles), shaped(*shape))(rate, field)
    return call(functools.partial(last_kernel, tiles), shaped(*shape))(rate, alpha, own, *received)


def solution(mesh):
    return jax.shard_map(
        per_device,
        mesh=mesh,
        in_specs=(
            P("mem", None, "tile", None),
            P("mem", None, None, "tile", None),
            P(),
            P("tile", None),
            P("tile", None),
            P("tile", None, None),
            P("tile", None),
            P("tile", None),
        ),
        out_specs=P("mem", None, "tile", None),
        check_vma=False,
    )
```

```python
import functools
import math

import jax
import jax.numpy as jnp
from jax import lax
from jax.experimental import pallas as pl
from jax.experimental.pallas import tpu as pltpu
from jax.sharding import PartitionSpec as P

F32 = jnp.float32
BF16 = jnp.bfloat16
I32 = jnp.int32
F8 = jnp.float8_e4m3fn
PIECES = 3
LANES = 128
Z_DECAY = math.exp(-1.0 / 3.0)
Z_GAIN = (1.0 - Z_DECAY) ** 2 * math.sqrt((1.0 + Z_DECAY) / (1.0 - Z_DECAY))
VMEM = pl.BlockSpec(memory_space=pltpu.VMEM)
COST = pl.CostEstimate(flops=2 * 10**10, bytes_accessed=4 * 10**6, transcendentals=0)
WIDE = pltpu.CompilerParams(vmem_limit_bytes=65000 * 1024)
PARAMS = pltpu.CompilerParams(vmem_limit_bytes=48 * 1024 * 1024)


def split(x):
    high = x.astype(BF16)
    return high, (x - high.astype(F32)).astype(BF16)


def dot(a, b):
    return jnp.dot(a, b, preferred_element_type=F32)


def dot3(a, b):
    (ah, al), (bh, bl) = split(a), split(b)
    return dot(ah, bh) + (dot(ah, bl) + dot(al, bh))


def iota(shape, dim):
    return lax.broadcasted_iota(I32, shape, dim)


def norm_of(rate):
    x = -rate
    series = jnp.ones_like(x)
    for k in (8, 7, 6, 5, 4, 3, 2):
        series = 1.0 - series * x * (1.0 / k)
    return jnp.sqrt(x * series / (1.0 + jnp.exp(rate)))


def pack_rays_kernel(per, *refs):
    given, (out_ref, rate_ref), held, sems = refs[:6], refs[6:8], refs[8:14], refs[14]
    copies = [pltpu.make_async_copy(given[k], held[k], sems.at[k]) for k in range(6)]
    for copy in copies:
        copy.start()
    for copy in copies:
        copy.wait()
    owner_ref, scales_ref, held = held[0], held[1], held[2:]
    levels = rate_ref.shape[0]
    here = iota((levels, levels), 0) == iota((levels, levels), 1)
    scale = jnp.sum(jnp.where(here, scales_ref[...], 0.0), axis=1, keepdims=True)
    rate_ref[...] = -1.0 / jnp.broadcast_to(scale, rate_ref.shape)
    rays, gates = held[0].shape
    tiles, halves = out_ref.shape[0], gates // LANES
    row = iota((tiles * per, rays), 0)
    target, wanted = row // per, row % per
    named = owner_ref[...] == target
    earlier = (iota((rays, rays), 0) < iota((rays, rays), 1)).astype(F32)
    rank = dot(named.astype(F32), earlier).astype(I32)
    picks = jnp.concatenate(
        [(named & (rank * halves + half == wanted)).astype(F32) for half in range(halves)], axis=1
    )
    cell_ref, weights_ref, observed_ref, precision_ref = held
    fields = (
        cell_ref[...].astype(F32),
        weights_ref[:, 0, :],
        weights_ref[:, 1, :],
        observed_ref[...],
        precision_ref[...],
    )
    stacked = jnp.concatenate(
        [
            jnp.concatenate([field[:, h * LANES : (h + 1) * LANES] for h in range(halves)], axis=0)
            for field in fields
        ],
        axis=1,
    )
    got = jnp.dot(picks, stacked, precision=lax.Precision.HIGHEST, preferred_element_type=F32)
    for t in range(tiles):
        for f in range(len(fields)):
            out_ref[t, f * per : (f + 1) * per] = got[t * per : (t + 1) * per, f * LANES : (f + 1) * LANES]


def filter_levels(field_ref, out_ref):
    levels = field_ref.shape[1]
    state = field_ref[:, 0]
    out_ref[:, 0] = state
    for l in range(1, levels):
        state = field_ref[:, l] + Z_DECAY * state
        out_ref[:, l] = state
    for l in range(levels - 2, -1, -1):
        state = out_ref[:, l] + Z_DECAY * state
        out_ref[:, l] = state


def filter_columns(field_ref, high_ref, low_ref, out_ref):
    members, levels, rows, columns = field_ref.shape

    def level(l, _):
        field = field_ref[:, l].reshape(members * rows, columns)
        high, low = split(field)
        both = dot(jnp.concatenate([high, low], axis=0), high_ref[l])
        total = both[: members * rows] + (both[members * rows :] + dot(high, low_ref[l]))
        out_ref[:, l] = total.reshape(members, rows, columns)
        return 0

    lax.fori_loop(0, levels, level, 0, unroll=4)


def columns_matrix(rate_ref, high_ref, low_ref):
    levels, n, _ = high_ref.shape
    i, j = iota((n, n), 0), iota((n, n), 1)
    dist = jnp.abs(i - j).astype(F32)
    left = (2 * (n - jnp.maximum(i, j))).astype(F32)

    def level(l, _):
        rate = rate_ref[pl.ds(l, 1), :]
        matrix = (Z_GAIN * norm_of(rate)) * jnp.exp(rate * dist) * (1.0 - jnp.exp(rate * left))
        high_ref[l], low_ref[l] = split(matrix)
        return 0

    lax.fori_loop(0, levels, level, 0, unroll=2)


def states(tiles, rate_ref, field_ref, out_ref):
    members, levels, rows, columns = field_ref.shape
    place = lax.axis_index("tile")
    per = LANES // rows
    level, column = iota((per, LANES), 0), iota((per, LANES), 1)
    same = level == column // rows
    at = (column % rows).astype(F32)
    left = (2 * (rows * tiles - rows * place) - 2 * (column % rows)).astype(F32)
    for g in range(levels // per):
        rate = rate_ref[g * per : (g + 1) * per]
        norm = norm_of(rate)
        forward = jnp.where(same, norm * jnp.exp(rate * (rows - 1.0 - at)), 0.0)
        backward = jnp.where(same, norm * jnp.exp(rate * at) * (1.0 - jnp.exp(rate * left)), 0.0)
        both = jnp.concatenate([forward, backward], axis=0)
        for b in range(members):
            field = field_ref[b, g * per : (g + 1) * per].reshape(per * rows, columns)
            got = dot3(both, field)
            for way in range(2):
                out_ref[way, b, g * per : (g + 1) * per] = got[way * per : (way + 1) * per]


def chip_kernel(tiles, rows, rate_ref, own_ref, partner_ref, *outs):
    place = lax.axis_index("tile")
    chip, upper, chips = place // 2, place % 2 == 1, tiles // 2
    members = own_ref.shape[1]
    across = jnp.exp(rate_ref[...] * rows)
    for b in range(members):
        first = [jnp.where(upper, partner_ref[way, b], own_ref[way, b]) for way in range(2)]
        second = [jnp.where(upper, own_ref[way, b], partner_ref[way, b]) for way in range(2)]
        forward = across * first[0] + second[0]
        backward = first[1] + across * second[1]
        for k in range(1, chips):
            outs[k - 1][b] = jnp.where(chip + k < chips, forward, backward)


def first_kernel(tiles, rate_ref, alpha_ref, high_ref, low_ref, out_ref, state_ref, scratch):
    columns_matrix(rate_ref, high_ref, low_ref)
    filter_levels(alpha_ref, scratch)
    filter_columns(scratch, high_ref, low_ref, out_ref)
    states(tiles, rate_ref, out_ref, state_ref)


def within_kernel(tiles, rate_ref, field_ref, out_ref):
    members, levels, rows, columns = field_ref.shape
    place = lax.axis_index("tile")
    per = LANES // rows
    n = per * rows
    row, column = iota((n, n), 0), iota((n, n), 1)
    same = row // rows == column // rows
    i, j = row % rows, column % rows
    dist = jnp.abs(i - j).astype(F32)
    left = (2 * (rows * tiles - rows * place) - 2 * jnp.maximum(i, j)).astype(F32)
    for g in range(levels // per):
        rate = jnp.concatenate(
            [jnp.broadcast_to(rate_ref[l : l + 1], (rows, LANES)) for l in range(g * per, (g + 1) * per)], axis=0
        )
        matrix = jnp.where(same, norm_of(rate) * jnp.exp(rate * dist) * (1.0 - jnp.exp(rate * left)), 0.0)
        for b in range(members):
            field = field_ref[b, g * per : (g + 1) * per].reshape(n, columns)
            out_ref[b, g * per : (g + 1) * per] = dot3(matrix, field).reshape(per, rows, columns)


def add_others(tiles, rate_ref, own_ref, received, out_ref, extra_ref=None):
    members, levels, rows, columns = own_ref.shape
    partner_ref, received = received[0], received[1:]
    place = lax.axis_index("tile")
    chip, upper, chips = place // 2, place % 2, tiles // 2
    rate = rate_ref[...]
    below = [jnp.where(upper == 1, partner_ref[0, b], 0.0) for b in range(members)]
    above = [jnp.where(upper == 0, partner_ref[1, b], 0.0) for b in range(members)]
    for k in range(1, chips):
        up = jnp.where(chip >= k, jnp.exp(rate * (rows * (2 * (k - 1) + upper)).astype(F32)), 0.0)
        down = jnp.where(chip < k, jnp.exp(rate * (rows * (2 * (chips - k) - 1 - upper)).astype(F32)), 0.0)
        for b in range(members):
            below[b] = below[b] + up * received[k - 1][b]
            above[b] = above[b] + down * received[k - 1][b]
    i = iota((rows, columns), 0)
    at = i.astype(F32)
    left = (2 * (rows * tiles - rows * place) - 2 * i).astype(F32)
    for l in range(levels):
        r = rate_ref[l : l + 1]
        from_below = jnp.exp(r * (at + 1.0)) * (1.0 - jnp.exp(r * left))
        from_above = jnp.exp(r * (rows - at))
        for b in range(members):
            total = own_ref[b, l] + (from_below * below[b][l : l + 1] + from_above * above[b][l : l + 1])
            out_ref[b, l] = total if extra_ref is None else total + extra_ref[b, l]


def indices(cells):
    whole = (cells + 0.5).astype(I32)
    return whole >> 7, whole & (LANES - 1)


def chunks_of(count):
    def run(body):
        def step(c, _):
            body(pl.ds(pl.multiple_of(c * 8, 8), 8))
            return 0

        lax.fori_loop(0, count // 8, step, 0, unroll=math.gcd(count // 8, 24))

    return run


def hot_rows(high, row_of, high_rows):
    count, _ = row_of.shape
    one, zero = jnp.ones((), BF16), jnp.zeros((), BF16)
    high = high.astype(F32)
    blocks = high_rows // count

    def rows(r):
        line = high[r : r + 1]
        return jnp.concatenate(
            [jnp.where(row_of == (line - float(count * h)).astype(BF16), one, zero) for h in range(blocks)], axis=0
        )

    return rows


def gather_kernel(tiles, per, rate_ref, own_ref, members_ref, *rest):
    received, rays = rest[: tiles // 2], rest[tiles // 2]
    out_ref, ray_ref, smooth_ref, table_ref = rest[tiles // 2 + 1 :]
    for s in range(tiles):
        for f in range(5):
            ray_ref[f, s * per : (s + 1) * per] = rays[s, f * per : (f + 1) * per]
    add_others(tiles, rate_ref, own_ref, received, smooth_ref)
    members, levels, rows, columns = own_ref.shape
    high_rows = levels * rows
    shares = []
    for f in range(2):
        share = jnp.zeros((high_rows, columns), F32)
        for b in range(members):
            share = share + members_ref[b, f].reshape(high_rows, columns).astype(F32) * smooth_ref[b].reshape(
                high_rows, columns
            )
        shares.append(share)
    largest = jnp.maximum(jnp.max(jnp.maximum(jnp.abs(shares[0]), jnp.abs(shares[1]))), 1e-30)
    scale, back = 256.0 / largest, largest * (1.0 / 256.0)
    for f in range(2):
        rest_of = shares[f].T * scale
        for k in range(PIECES):
            piece = rest_of.astype(F8)
            table_ref[(2 * k + f) * LANES : (2 * k + f + 1) * LANES] = piece
            rest_of = (rest_of - piece.astype(F32)) * 16.0
    row_of = iota((256, LANES), 0).astype(F32).astype(BF16)
    lane_of = iota((LANES, LANES), 0)

    @chunks_of(out_ref.shape[0])
    def _(at):
        high, low = indices(ray_ref[0, at, :])
        hot_row = hot_rows(high, row_of, high_rows)
        first, second = ray_ref[1, at, :] * back, ray_ref[2, at, :] * back
        lines = []
        for pair in range(4):
            hot = jnp.concatenate([hot_row(2 * pair), hot_row(2 * pair + 1)], axis=1).astype(F8)
            got = dot(table_ref[...], hot)
            total = got[: 2 * LANES]
            for k in range(1, PIECES):
                total = total + got[2 * k * LANES : 2 * (k + 1) * LANES] * 16.0**-k
            for h in range(2):
                r = 2 * pair + h
                here = lane_of == low[r : r + 1]
                part = total[:, h * LANES : (h + 1) * LANES]
                u = jnp.sum(jnp.where(here, part[:LANES], 0.0), axis=0, keepdims=True)
                v = jnp.sum(jnp.where(here, part[LANES:], 0.0), axis=0, keepdims=True)
                lines.append(u * first[r : r + 1] + v * second[r : r + 1])
        out_ref[at, :] = jnp.concatenate(lines, axis=0)


def scatter_kernel(tiles, blocks, rate_ref, high_ref, low_ref, members_ref, ray_ref, *rest):
    partial, (out_ref, state_ref, total_ref, mixed_ref, value_ref) = rest[:blocks], rest[blocks:]
    modelled = partial[0][...]
    for other in partial[1:]:
        modelled = modelled + other[...]
    departure = ray_ref[4] * (modelled - ray_ref[3])
    given = [ray_ref[1 + f] * departure for f in range(2)]
    largest = jnp.maximum(jnp.max(jnp.maximum(jnp.abs(given[0]), jnp.abs(given[1]))), 1e-30)
    scale, back = 256.0 / largest, largest * (1.0 / 256.0)
    for f in range(2):
        value_ref[f] = given[f] * scale
    members, levels, rows, columns = out_ref.shape
    high_rows = levels * rows
    row_of = iota((256, LANES), 0).astype(F32).astype(BF16)
    lane_of = iota((LANES, LANES), 0).astype(F32).astype(BF16)
    none = jnp.zeros((), BF16)
    total_ref[...] = jnp.zeros_like(total_ref)

    @chunks_of(ray_ref.shape[1])
    def _(at):
        high, low = indices(ray_ref[0, at, :])
        hot_row = hot_rows(high, row_of, high_rows)
        low = low.astype(F32)
        pieces = []
        rest_of = [value_ref[f, at, :] for f in range(2)]
        for _ in range(PIECES):
            for f in range(2):
                piece = rest_of[f].astype(F8).astype(F32)
                rest_of[f] = (rest_of[f] - piece) * 16.0
                pieces.append(piece)
        sides = []
        for r in range(8):
            here = lane_of == low[r : r + 1].astype(BF16)
            sides.append(
                jnp.concatenate(
                    [jnp.where(here, piece[r : r + 1].astype(BF16), none) for piece in pieces], axis=0
                ).astype(F8)
            )
        total_ref[...] += lax.dot_general(
            jnp.concatenate([hot_row(r).astype(F8) for r in range(8)], axis=1),
            jnp.concatenate(sides, axis=1),
            (((1,), (1,)), ((), ())),
            preferred_element_type=F32,
        )

    for l in range(levels):
        total = total_ref[l * rows : (l + 1) * rows]
        both = total[:, : 2 * LANES]
        for k in range(1, PIECES):
            both = both + total[:, 2 * k * LANES : 2 * (k + 1) * LANES] * 16.0**-k
        u, v = both[:, :LANES] * back, both[:, LANES:] * back
        for b in range(members):
            mixed_ref[b, l] = members_ref[b, 0, l].astype(F32) * u + members_ref[b, 1, l].astype(F32) * v
    filter_levels(mixed_ref, mixed_ref)
    filter_columns(mixed_ref, high_ref, low_ref, out_ref)
    states(tiles, rate_ref, out_ref, state_ref)


def last_kernel(tiles, rate_ref, alpha_ref, own_ref, *rest):
    add_others(tiles, rate_ref, own_ref, rest[:-1], rest[-1], alpha_ref)


def call(body, outs, scratch=(), cost=None, specs=None, params=PARAMS):
    def run(*args):
        return pl.pallas_call(
            body,
            out_shape=outs,
            in_specs=specs or [VMEM] * len(args),
            out_specs=jax.tree.map(lambda _: VMEM, outs),
            scratch_shapes=list(scratch),
            compiler_params=params,
            cost_estimate=cost,
        )(*args)

    return run


def shaped(*shape, dtype=F32):
    return jax.ShapeDtypeStruct(shape, dtype)


def over_members(part, blocks):
    return [lax.ppermute(part, "mem", [(i, i ^ k) for i in range(blocks)]) for k in range(1, blocks)]


def exchange(rate, own, rows, tiles):
    chips = tiles // 2
    partner = lax.ppermute(own, "tile", [(i, i ^ 1) for i in range(tiles)])
    given = call(functools.partial(chip_kernel, tiles, rows), [shaped(*own.shape[1:])] * (chips - 1))(
        rate, own, partner
    )
    return [
        partner,
        *(
            lax.ppermute(
                part, "tile", [(2 * c + h, 2 * ((c + k) % chips) + h) for c in range(chips) for h in range(2)]
            )
            for k, part in enumerate(given, 1)
        ),
    ]


def per_device(alpha, members, scales, observed, precision, ray_weights, cell_index, owner):
    tiles, blocks = lax.axis_size("tile"), lax.axis_size("mem")
    count_rays, gates = observed.shape
    capacity = 3 * count_rays // tiles
    per = capacity * (gates // LANES)
    shape = alpha.shape
    count, levels, rows, columns = shape
    anywhere = pl.BlockSpec(memory_space=pltpu.HBM)
    given = (
        owner.reshape(1, count_rays),
        scales.reshape(1, levels),
        cell_index,
        ray_weights,
        observed,
        precision,
    )
    sent, rate = call(
        functools.partial(pack_rays_kernel, per),
        [shaped(tiles, 5 * per, LANES), shaped(levels, LANES)],
        [*(pltpu.VMEM(x.shape, x.dtype) for x in given), pltpu.SemaphoreType.DMA((6,))],
        specs=[anywhere] * 6,
        params=WIDE,
    )(*given)
    here = lax.all_to_all(sent, "tile", split_axis=0, concat_axis=0, tiled=True)

    state = shaped(2, count, levels, columns)
    high, low, field, own = call(
        functools.partial(first_kernel, tiles),
        [shaped(levels, columns, columns, dtype=BF16)] * 2 + [shaped(*shape), state],
        [pltpu.VMEM(shape, F32)],
    )(rate, alpha)
    received = exchange(rate, own, rows, tiles)
    own = call(functools.partial(within_kernel, tiles), shaped(*shape))(rate, field)
    total = tiles * per
    modelled, ray = call(
        functools.partial(gather_kernel, tiles, per),
        [shaped(total, LANES), shaped(5, total, LANES)],
        [pltpu.VMEM(shape, F32), pltpu.VMEM((2 * PIECES * LANES, levels * rows), F8)],
        COST,
    )(rate, own, members, *received, here)
    field, own = call(
        functools.partial(scatter_kernel, tiles, blocks),
        [shaped(*shape), state],
        [
            pltpu.VMEM((levels * rows, 2 * PIECES * LANES), F32),
            pltpu.VMEM(shape, F32),
            pltpu.VMEM((2, total, LANES), F32),
        ],
        COST,
    )(rate, high, low, members, ray, modelled, *over_members(modelled, blocks))
    received = exchange(rate, own, rows, tiles)
    own = call(functools.partial(within_kernel, tiles), shaped(*shape))(rate, field)
    return call(functools.partial(last_kernel, tiles), shaped(*shape))(rate, alpha, own, *received)


def solution(mesh):
    return jax.shard_map(
        per_device,
        mesh=mesh,
        in_specs=(
            P("mem", None, "tile", None),
            P("mem", None, None, "tile", None),
            P(),
            P("tile", None),
            P("tile", None),
            P("tile", None, None),
            P("tile", None),
            P("tile", None),
        ),
        out_specs=P("mem", None, "tile", None),
        check_vma=False,
    )
```

```python
import functools
import math

import jax
import jax.numpy as jnp
from jax import lax
from jax.experimental import pallas as pl
from jax.experimental.pallas import tpu as pltpu
from jax.sharding import PartitionSpec as P

F32 = jnp.float32
BF16 = jnp.bfloat16
I32 = jnp.int32
F8 = jnp.float8_e4m3fn
PIECES = 3
LANES = 128
Z_DECAY = math.exp(-1.0 / 3.0)
Z_GAIN = (1.0 - Z_DECAY) ** 2 * math.sqrt((1.0 + Z_DECAY) / (1.0 - Z_DECAY))
VMEM = pl.BlockSpec(memory_space=pltpu.VMEM)
COST = pl.CostEstimate(flops=2 * 10**10, bytes_accessed=4 * 10**6, transcendentals=0)
WIDE = pltpu.CompilerParams(vmem_limit_bytes=65000 * 1024)
PARAMS = pltpu.CompilerParams(vmem_limit_bytes=48 * 1024 * 1024)


def split(x):
    high = x.astype(BF16)
    return high, (x - high.astype(F32)).astype(BF16)


def dot(a, b):
    return jnp.dot(a, b, preferred_element_type=F32)


def dot3(a, b):
    (ah, al), (bh, bl) = split(a), split(b)
    return dot(ah, bh) + (dot(ah, bl) + dot(al, bh))


def iota(shape, dim):
    return lax.broadcasted_iota(I32, shape, dim)


def norm_of(rate):
    x = -rate
    series = jnp.ones_like(x)
    for k in (8, 7, 6, 5, 4, 3, 2):
        series = 1.0 - series * x * (1.0 / k)
    return jnp.sqrt(x * series / (1.0 + jnp.exp(rate)))


def pack_rays_kernel(per, *refs):
    given, (out_ref, rate_ref), held, sems = refs[:6], refs[6:8], refs[8:14], refs[14]
    copies = [pltpu.make_async_copy(given[k], held[k], sems.at[k]) for k in range(6)]
    for copy in copies:
        copy.start()
    for copy in copies[:2]:
        copy.wait()
    owner_ref, scales_ref, held = held[0], held[1], held[2:]
    levels = rate_ref.shape[0]
    here = iota((levels, levels), 0) == iota((levels, levels), 1)
    scale = jnp.sum(jnp.where(here, scales_ref[...], 0.0), axis=1, keepdims=True)
    rate_ref[...] = -1.0 / jnp.broadcast_to(scale, rate_ref.shape)
    rays, gates = held[0].shape
    tiles, halves = out_ref.shape[0], gates // LANES
    row = iota((tiles * per, rays), 0)
    target, wanted = row // per, row % per
    named = owner_ref[...] == target
    earlier = (iota((rays, rays), 0) < iota((rays, rays), 1)).astype(F32)
    rank = dot(named.astype(F32), earlier).astype(I32)
    picks = jnp.concatenate(
        [(named & (rank * halves + half == wanted)).astype(F32).astype(BF16) for half in range(halves)], axis=1
    )
    for copy in copies[2:]:
        copy.wait()
    cell_ref, weights_ref, observed_ref, precision_ref = held
    fields = (
        cell_ref[...].astype(F32),
        weights_ref[:, 0, :],
        weights_ref[:, 1, :],
        observed_ref[...],
        precision_ref[...],
    )
    stacked = jnp.concatenate(
        [
            jnp.concatenate([field[:, h * LANES : (h + 1) * LANES] for h in range(halves)], axis=0)
            for field in fields
        ],
        axis=1,
    )
    high = stacked.astype(BF16)
    middle, low = split(stacked - high.astype(F32))
    got = dot(picks, high) + (dot(picks, middle) + dot(picks, low))
    for t in range(tiles):
        for f in range(len(fields)):
            out_ref[t, f * per : (f + 1) * per] = got[t * per : (t + 1) * per, f * LANES : (f + 1) * LANES]


def filter_levels(field_ref, out_ref):
    levels = field_ref.shape[1]
    state = field_ref[:, 0]
    out_ref[:, 0] = state
    for l in range(1, levels):
        state = field_ref[:, l] + Z_DECAY * state
        out_ref[:, l] = state
    for l in range(levels - 2, -1, -1):
        state = out_ref[:, l] + Z_DECAY * state
        out_ref[:, l] = state


def filter_columns(field_ref, high_ref, low_ref, out_ref):
    members, levels, rows, columns = field_ref.shape

    def level(l, _):
        field = field_ref[:, l].reshape(members * rows, columns)
        high, low = split(field)
        both = dot(jnp.concatenate([high, low], axis=0), high_ref[l])
        total = both[: members * rows] + (both[members * rows :] + dot(high, low_ref[l]))
        out_ref[:, l] = total.reshape(members, rows, columns)
        return 0

    lax.fori_loop(0, levels, level, 0, unroll=8)


def columns_matrix(rate_ref, high_ref, low_ref):
    levels, n, _ = high_ref.shape
    i, j = iota((n, n), 0), iota((n, n), 1)
    dist = jnp.abs(i - j).astype(F32)
    left = (2 * (n - jnp.maximum(i, j))).astype(F32)

    def level(l, _):
        rate = rate_ref[pl.ds(l, 1), :]
        matrix = (Z_GAIN * norm_of(rate)) * jnp.exp(rate * dist) * (1.0 - jnp.exp(rate * left))
        high_ref[l], low_ref[l] = split(matrix)
        return 0

    lax.fori_loop(0, levels, level, 0, unroll=8)


def states(tiles, rate_ref, field_ref, out_ref):
    members, levels, rows, columns = field_ref.shape
    place = lax.axis_index("tile")
    per = LANES // rows
    level, column = iota((per, LANES), 0), iota((per, LANES), 1)
    same = level == column // rows
    at = (column % rows).astype(F32)
    left = (2 * (rows * tiles - rows * place) - 2 * (column % rows)).astype(F32)
    for g in range(levels // per):
        rate = rate_ref[g * per : (g + 1) * per]
        norm = norm_of(rate)
        forward = jnp.where(same, norm * jnp.exp(rate * (rows - 1.0 - at)), 0.0)
        backward = jnp.where(same, norm * jnp.exp(rate * at) * (1.0 - jnp.exp(rate * left)), 0.0)
        both = jnp.concatenate([forward, backward], axis=0)
        for b in range(members):
            field = field_ref[b, g * per : (g + 1) * per].reshape(per * rows, columns)
            got = dot3(both, field)
            for way in range(2):
                out_ref[way, b, g * per : (g + 1) * per] = got[way * per : (way + 1) * per]


def chip_kernel(tiles, rows, rate_ref, own_ref, partner_ref, *outs):
    place = lax.axis_index("tile")
    chip, upper, chips = place // 2, place % 2 == 1, tiles // 2
    members = own_ref.shape[1]
    across = jnp.exp(rate_ref[...] * rows)
    for b in range(members):
        first = [jnp.where(upper, partner_ref[way, b], own_ref[way, b]) for way in range(2)]
        second = [jnp.where(upper, own_ref[way, b], partner_ref[way, b]) for way in range(2)]
        forward = across * first[0] + second[0]
        backward = first[1] + across * second[1]
        for k in range(1, chips):
            outs[k - 1][b] = jnp.where(chip + k < chips, forward, backward)


def first_kernel(tiles, rate_ref, alpha_ref, high_ref, low_ref, out_ref, state_ref, scratch):
    columns_matrix(rate_ref, high_ref, low_ref)
    filter_levels(alpha_ref, scratch)
    filter_columns(scratch, high_ref, low_ref, out_ref)
    states(tiles, rate_ref, out_ref, state_ref)


def within_kernel(tiles, rate_ref, field_ref, out_ref):
    members, levels, rows, columns = field_ref.shape
    place = lax.axis_index("tile")
    per = LANES // rows
    n = per * rows
    row, column = iota((n, n), 0), iota((n, n), 1)
    same = row // rows == column // rows
    i, j = row % rows, column % rows
    dist = jnp.abs(i - j).astype(F32)
    left = (2 * (rows * tiles - rows * place) - 2 * jnp.maximum(i, j)).astype(F32)
    for g in range(levels // per):
        rate = jnp.concatenate(
            [jnp.broadcast_to(rate_ref[l : l + 1], (rows, LANES)) for l in range(g * per, (g + 1) * per)], axis=0
        )
        matrix = jnp.where(same, norm_of(rate) * jnp.exp(rate * dist) * (1.0 - jnp.exp(rate * left)), 0.0)
        for b in range(members):
            field = field_ref[b, g * per : (g + 1) * per].reshape(n, columns)
            out_ref[b, g * per : (g + 1) * per] = dot3(matrix, field).reshape(per, rows, columns)


def add_others(tiles, rate_ref, own_ref, received, out_ref, extra_ref=None):
    members, levels, rows, columns = own_ref.shape
    partner_ref, received = received[0], received[1:]
    place = lax.axis_index("tile")
    chip, upper, chips = place // 2, place % 2, tiles // 2
    rate = rate_ref[...]
    below = [jnp.where(upper == 1, partner_ref[0, b], 0.0) for b in range(members)]
    above = [jnp.where(upper == 0, partner_ref[1, b], 0.0) for b in range(members)]
    for k in range(1, chips):
        up = jnp.where(chip >= k, jnp.exp(rate * (rows * (2 * (k - 1) + upper)).astype(F32)), 0.0)
        down = jnp.where(chip < k, jnp.exp(rate * (rows * (2 * (chips - k) - 1 - upper)).astype(F32)), 0.0)
        for b in range(members):
            below[b] = below[b] + up * received[k - 1][b]
            above[b] = above[b] + down * received[k - 1][b]
    i = iota((rows, columns), 0)
    at = i.astype(F32)
    left = (2 * (rows * tiles - rows * place) - 2 * i).astype(F32)
    for l in range(levels):
        r = rate_ref[l : l + 1]
        from_below = jnp.exp(r * (at + 1.0)) * (1.0 - jnp.exp(r * left))
        from_above = jnp.exp(r * (rows - at))
        for b in range(members):
            total = own_ref[b, l] + (from_below * below[b][l : l + 1] + from_above * above[b][l : l + 1])
            out_ref[b, l] = total if extra_ref is None else total + extra_ref[b, l]


def indices(cells):
    whole = (cells + 0.5).astype(I32)
    return whole >> 7, whole & (LANES - 1)


def chunks_of(count):
    def run(body):
        def step(c, _):
            body(pl.ds(pl.multiple_of(c * 8, 8), 8))
            return 0

        lax.fori_loop(0, count // 8, step, 0, unroll=math.gcd(count // 8, 24))

    return run


def hot_rows(high, row_of, high_rows):
    count, _ = row_of.shape
    one, zero = jnp.ones((), BF16), jnp.zeros((), BF16)
    high = high.astype(F32)
    blocks = high_rows // count

    def rows(r):
        line = high[r : r + 1]
        return jnp.concatenate(
            [jnp.where(row_of == (line - float(count * h)).astype(BF16), one, zero) for h in range(blocks)], axis=0
        )

    return rows


def gather_kernel(tiles, per, rate_ref, own_ref, members_ref, *rest):
    received, rays = rest[: tiles // 2], rest[tiles // 2]
    out_ref, ray_ref, smooth_ref, table_ref = rest[tiles // 2 + 1 :]
    for s in range(tiles):
        for f in range(5):
            ray_ref[f, s * per : (s + 1) * per] = rays[s, f * per : (f + 1) * per]
    add_others(tiles, rate_ref, own_ref, received, smooth_ref)
    members, levels, rows, columns = own_ref.shape
    high_rows = levels * rows
    shares = []
    for f in range(2):
        share = jnp.zeros((high_rows, columns), F32)
        for b in range(members):
            share = share + members_ref[b, f].reshape(high_rows, columns).astype(F32) * smooth_ref[b].reshape(
                high_rows, columns
            )
        shares.append(share)
    largest = jnp.maximum(jnp.max(jnp.maximum(jnp.abs(shares[0]), jnp.abs(shares[1]))), 1e-30)
    scale, back = 256.0 / largest, largest * (1.0 / 256.0)
    for f in range(2):
        rest_of = shares[f].T * scale
        for k in range(PIECES):
            piece = rest_of.astype(F8)
            table_ref[(2 * k + f) * LANES : (2 * k + f + 1) * LANES] = piece
            rest_of = (rest_of - piece.astype(F32)) * 16.0
    row_of = iota((256, LANES), 0).astype(F32).astype(BF16)
    lane_of = iota((LANES, LANES), 0)

    @chunks_of(out_ref.shape[0])
    def _(at):
        high, low = indices(ray_ref[0, at, :])
        hot_row = hot_rows(high, row_of, high_rows)
        first, second = ray_ref[1, at, :] * back, ray_ref[2, at, :] * back
        lines = []
        for pair in range(4):
            hot = jnp.concatenate([hot_row(2 * pair), hot_row(2 * pair + 1)], axis=1).astype(F8)
            got = dot(table_ref[...], hot)
            total = got[: 2 * LANES]
            for k in range(1, PIECES):
                total = total + got[2 * k * LANES : 2 * (k + 1) * LANES] * 16.0**-k
            for h in range(2):
                r = 2 * pair + h
                here = lane_of == low[r : r + 1]
                part = total[:, h * LANES : (h + 1) * LANES]
                u = jnp.sum(jnp.where(here, part[:LANES], 0.0), axis=0, keepdims=True)
                v = jnp.sum(jnp.where(here, part[LANES:], 0.0), axis=0, keepdims=True)
                lines.append(u * first[r : r + 1] + v * second[r : r + 1])
        out_ref[at, :] = jnp.concatenate(lines, axis=0)


def scatter_kernel(tiles, blocks, rate_ref, high_ref, low_ref, members_ref, ray_ref, *rest):
    partial, (out_ref, state_ref, total_ref, mixed_ref, value_ref) = rest[:blocks], rest[blocks:]
    modelled = partial[0][...]
    for other in partial[1:]:
        modelled = modelled + other[...]
    departure = ray_ref[4] * (modelled - ray_ref[3])
    given = [ray_ref[1 + f] * departure for f in range(2)]
    largest = jnp.maximum(jnp.max(jnp.maximum(jnp.abs(given[0]), jnp.abs(given[1]))), 1e-30)
    scale, back = 256.0 / largest, largest * (1.0 / 256.0)
    for f in range(2):
        value_ref[f] = given[f] * scale
    members, levels, rows, columns = out_ref.shape
    high_rows = levels * rows
    row_of = iota((256, LANES), 0).astype(F32).astype(BF16)
    lane_of = iota((LANES, LANES), 0).astype(F32).astype(BF16)
    none = jnp.zeros((), BF16)
    total_ref[...] = jnp.zeros_like(total_ref)

    @chunks_of(ray_ref.shape[1])
    def _(at):
        high, low = indices(ray_ref[0, at, :])
        hot_row = hot_rows(high, row_of, high_rows)
        low = low.astype(F32)
        pieces = []
        rest_of = [value_ref[f, at, :] for f in range(2)]
        for _ in range(PIECES):
            for f in range(2):
                piece = rest_of[f].astype(F8).astype(F32)
                rest_of[f] = (rest_of[f] - piece) * 16.0
                pieces.append(piece)
        sides = []
        for r in range(8):
            here = lane_of == low[r : r + 1].astype(BF16)
            sides.append(
                jnp.concatenate(
                    [jnp.where(here, piece[r : r + 1].astype(BF16), none) for piece in pieces], axis=0
                ).astype(F8)
            )
        total_ref[...] += lax.dot_general(
            jnp.concatenate([hot_row(r).astype(F8) for r in range(8)], axis=1),
            jnp.concatenate(sides, axis=1),
            (((1,), (1,)), ((), ())),
            preferred_element_type=F32,
        )

    for l in range(levels):
        total = total_ref[l * rows : (l + 1) * rows]
        both = total[:, : 2 * LANES]
        for k in range(1, PIECES):
            both = both + total[:, 2 * k * LANES : 2 * (k + 1) * LANES] * 16.0**-k
        u, v = both[:, :LANES] * back, both[:, LANES:] * back
        for b in range(members):
            mixed_ref[b, l] = members_ref[b, 0, l].astype(F32) * u + members_ref[b, 1, l].astype(F32) * v
    filter_levels(mixed_ref, mixed_ref)
    filter_columns(mixed_ref, high_ref, low_ref, out_ref)
    states(tiles, rate_ref, out_ref, state_ref)


def last_kernel(tiles, rate_ref, alpha_ref, own_ref, *rest):
    add_others(tiles, rate_ref, own_ref, rest[:-1], rest[-1], alpha_ref)


def call(body, outs, scratch=(), cost=None, specs=None, params=PARAMS):
    def run(*args):
        return pl.pallas_call(
            body,
            out_shape=outs,
            in_specs=specs or [VMEM] * len(args),
            out_specs=jax.tree.map(lambda _: VMEM, outs),
            scratch_shapes=list(scratch),
            compiler_params=params,
            cost_estimate=cost,
        )(*args)

    return run


def shaped(*shape, dtype=F32):
    return jax.ShapeDtypeStruct(shape, dtype)


def over_members(part, blocks):
    return [lax.ppermute(part, "mem", [(i, i ^ k) for i in range(blocks)]) for k in range(1, blocks)]


def exchange(rate, own, rows, tiles):
    chips = tiles // 2
    partner = lax.ppermute(own, "tile", [(i, i ^ 1) for i in range(tiles)])
    given = call(functools.partial(chip_kernel, tiles, rows), [shaped(*own.shape[1:])] * (chips - 1))(
        rate, own, partner
    )
    return [
        partner,
        *(
            lax.ppermute(
                part, "tile", [(2 * c + h, 2 * ((c + k) % chips) + h) for c in range(chips) for h in range(2)]
            )
            for k, part in enumerate(given, 1)
        ),
    ]


def per_device(alpha, members, scales, observed, precision, ray_weights, cell_index, owner):
    tiles, blocks = lax.axis_size("tile"), lax.axis_size("mem")
    count_rays, gates = observed.shape
    capacity = 3 * count_rays // tiles
    per = capacity * (gates // LANES)
    shape = alpha.shape
    count, levels, rows, columns = shape
    anywhere = pl.BlockSpec(memory_space=pltpu.HBM)
    given = (
        owner.reshape(1, count_rays),
        scales.reshape(1, levels),
        cell_index,
        ray_weights,
        observed,
        precision,
    )
    sent, rate = call(
        functools.partial(pack_rays_kernel, per),
        [shaped(tiles, 5 * per, LANES), shaped(levels, LANES)],
        [*(pltpu.VMEM(x.shape, x.dtype) for x in given), pltpu.SemaphoreType.DMA((6,))],
        specs=[anywhere] * 6,
        params=WIDE,
    )(*given)
    here = lax.all_to_all(sent, "tile", split_axis=0, concat_axis=0, tiled=True)

    state = shaped(2, count, levels, columns)
    high, low, field, own = call(
        functools.partial(first_kernel, tiles),
        [shaped(levels, columns, columns, dtype=BF16)] * 2 + [shaped(*shape), state],
        [pltpu.VMEM(shape, F32)],
    )(rate, alpha)
    received = exchange(rate, own, rows, tiles)
    own = call(functools.partial(within_kernel, tiles), shaped(*shape))(rate, field)
    total = tiles * per
    modelled, ray = call(
        functools.partial(gather_kernel, tiles, per),
        [shaped(total, LANES), shaped(5, total, LANES)],
        [pltpu.VMEM(shape, F32), pltpu.VMEM((2 * PIECES * LANES, levels * rows), F8)],
        COST,
    )(rate, own, members, *received, here)
    field, own = call(
        functools.partial(scatter_kernel, tiles, blocks),
        [shaped(*shape), state],
        [
            pltpu.VMEM((levels * rows, 2 * PIECES * LANES), F32),
            pltpu.VMEM(shape, F32),
            pltpu.VMEM((2, total, LANES), F32),
        ],
        COST,
    )(rate, high, low, members, ray, modelled, *over_members(modelled, blocks))
    received = exchange(rate, own, rows, tiles)
    own = call(functools.partial(within_kernel, tiles), shaped(*shape))(rate, field)
    return call(functools.partial(last_kernel, tiles), shaped(*shape))(rate, alpha, own, *received)


def solution(mesh):
    return jax.shard_map(
        per_device,
        mesh=mesh,
        in_specs=(
            P("mem", None, "tile", None),
            P("mem", None, None, "tile", None),
            P(),
            P("tile", None),
            P("tile", None),
            P("tile", None, None),
            P("tile", None),
            P("tile", None),
        ),
        out_specs=P("mem", None, "tile", None),
        check_vma=False,
    )
```

```python
import functools
import math

import jax
import jax.numpy as jnp
from jax import lax
from jax.experimental import pallas as pl
from jax.experimental.pallas import tpu as pltpu
from jax.sharding import PartitionSpec as P

F32 = jnp.float32
BF16 = jnp.bfloat16
I32 = jnp.int32
F8 = jnp.float8_e4m3fn
PIECES = 3
LANES = 128
Z_DECAY = math.exp(-1.0 / 3.0)
Z_GAIN = (1.0 - Z_DECAY) ** 2 * math.sqrt((1.0 + Z_DECAY) / (1.0 - Z_DECAY))
VMEM = pl.BlockSpec(memory_space=pltpu.VMEM)
COST = pl.CostEstimate(flops=2 * 10**10, bytes_accessed=4 * 10**6, transcendentals=0)
WIDE = pltpu.CompilerParams(vmem_limit_bytes=65000 * 1024)
PARAMS = pltpu.CompilerParams(vmem_limit_bytes=48 * 1024 * 1024)


def split(x):
    high = x.astype(BF16)
    return high, (x - high.astype(F32)).astype(BF16)


def dot(a, b):
    return jnp.dot(a, b, preferred_element_type=F32)


def dot3(a, b):
    (ah, al), (bh, bl) = split(a), split(b)
    return dot(ah, bh) + (dot(ah, bl) + dot(al, bh))


def iota(shape, dim):
    return lax.broadcasted_iota(I32, shape, dim)


def norm_of(rate):
    x = -rate
    series = jnp.ones_like(x)
    for k in (8, 7, 6, 5, 4, 3, 2):
        series = 1.0 - series * x * (1.0 / k)
    return jnp.sqrt(x * series / (1.0 + jnp.exp(rate)))


def pack_rays_kernel(per, *refs):
    given, (out_ref, rate_ref), held, sems = refs[:6], refs[6:8], refs[8:14], refs[14]
    copies = [pltpu.make_async_copy(given[k], held[k], sems.at[k]) for k in range(6)]
    for copy in copies:
        copy.start()
    for copy in copies[:2]:
        copy.wait()
    owner_ref, scales_ref, held = held[0], held[1], held[2:]
    levels = rate_ref.shape[0]
    here = iota((levels, levels), 0) == iota((levels, levels), 1)
    scale = jnp.sum(jnp.where(here, scales_ref[...], 0.0), axis=1, keepdims=True)
    rate_ref[...] = -1.0 / jnp.broadcast_to(scale, rate_ref.shape)
    rays, gates = held[0].shape
    tiles, halves = out_ref.shape[0], gates // LANES
    row = iota((tiles * per, rays), 0)
    target, wanted = row // per, row % per
    named = owner_ref[...] == target
    earlier = (iota((rays, rays), 0) < iota((rays, rays), 1)).astype(F32)
    rank = dot(named.astype(F32), earlier).astype(I32)
    picks = jnp.concatenate(
        [(named & (rank * halves + half == wanted)).astype(F32).astype(BF16) for half in range(halves)], axis=1
    )
    for copy in copies[2:]:
        copy.wait()
    cell_ref, weights_ref, observed_ref, precision_ref = held
    fields = (
        cell_ref[...].astype(F32),
        weights_ref[:, 0, :],
        weights_ref[:, 1, :],
        observed_ref[...],
        precision_ref[...],
    )
    stacked = jnp.concatenate(
        [
            jnp.concatenate([field[:, h * LANES : (h + 1) * LANES] for h in range(halves)], axis=0)
            for field in fields
        ],
        axis=1,
    )
    high = stacked.astype(BF16)
    middle, low = split(stacked - high.astype(F32))
    got = dot(picks, high) + (dot(picks, middle) + dot(picks, low))
    for t in range(tiles):
        for f in range(len(fields)):
            out_ref[t, f * per : (f + 1) * per] = got[t * per : (t + 1) * per, f * LANES : (f + 1) * LANES]


def filter_levels(field_ref, out_ref):
    levels = field_ref.shape[1]
    state = field_ref[:, 0]
    out_ref[:, 0] = state
    for l in range(1, levels):
        state = field_ref[:, l] + Z_DECAY * state
        out_ref[:, l] = state
    for l in range(levels - 2, -1, -1):
        state = out_ref[:, l] + Z_DECAY * state
        out_ref[:, l] = state


def filter_columns(field_ref, high_ref, low_ref, out_ref):
    members, levels, rows, columns = field_ref.shape

    def level(l, _):
        field = field_ref[:, l].reshape(members * rows, columns)
        high, low = split(field)
        both = dot(jnp.concatenate([high, low], axis=0), high_ref[l])
        total = both[: members * rows] + (both[members * rows :] + dot(high, low_ref[l]))
        out_ref[:, l] = total.reshape(members, rows, columns)
        return 0

    lax.fori_loop(0, levels, level, 0, unroll=16)


def columns_matrix(rate_ref, high_ref, low_ref):
    levels, n, _ = high_ref.shape
    i, j = iota((n, n), 0), iota((n, n), 1)
    dist = jnp.abs(i - j).astype(F32)
    left = (2 * (n - jnp.maximum(i, j))).astype(F32)

    def level(l, _):
        rate = rate_ref[pl.ds(l, 1), :]
        matrix = (Z_GAIN * norm_of(rate)) * jnp.exp(rate * dist) * (1.0 - jnp.exp(rate * left))
        high_ref[l], low_ref[l] = split(matrix)
        return 0

    lax.fori_loop(0, levels, level, 0, unroll=16)


def states(tiles, rate_ref, field_ref, out_ref):
    members, levels, rows, columns = field_ref.shape
    place = lax.axis_index("tile")
    per = LANES // rows
    level, column = iota((per, LANES), 0), iota((per, LANES), 1)
    same = level == column // rows
    at = (column % rows).astype(F32)
    left = (2 * (rows * tiles - rows * place) - 2 * (column % rows)).astype(F32)
    for g in range(levels // per):
        rate = rate_ref[g * per : (g + 1) * per]
        norm = norm_of(rate)
        forward = jnp.where(same, norm * jnp.exp(rate * (rows - 1.0 - at)), 0.0)
        backward = jnp.where(same, norm * jnp.exp(rate * at) * (1.0 - jnp.exp(rate * left)), 0.0)
        both = jnp.concatenate([forward, backward], axis=0)
        for b in range(members):
            field = field_ref[b, g * per : (g + 1) * per].reshape(per * rows, columns)
            got = dot3(both, field)
            for way in range(2):
                out_ref[way, b, g * per : (g + 1) * per] = got[way * per : (way + 1) * per]


def chip_kernel(tiles, rows, rate_ref, own_ref, partner_ref, *outs):
    place = lax.axis_index("tile")
    chip, upper, chips = place // 2, place % 2 == 1, tiles // 2
    members = own_ref.shape[1]
    across = jnp.exp(rate_ref[...] * rows)
    for b in range(members):
        first = [jnp.where(upper, partner_ref[way, b], own_ref[way, b]) for way in range(2)]
        second = [jnp.where(upper, own_ref[way, b], partner_ref[way, b]) for way in range(2)]
        forward = across * first[0] + second[0]
        backward = first[1] + across * second[1]
        for k in range(1, chips):
            outs[k - 1][b] = jnp.where(chip + k < chips, forward, backward)


def first_kernel(tiles, rate_ref, alpha_ref, high_ref, low_ref, out_ref, state_ref, scratch):
    columns_matrix(rate_ref, high_ref, low_ref)
    filter_levels(alpha_ref, scratch)
    filter_columns(scratch, high_ref, low_ref, out_ref)
    states(tiles, rate_ref, out_ref, state_ref)


def within_kernel(tiles, rate_ref, field_ref, out_ref):
    members, levels, rows, columns = field_ref.shape
    place = lax.axis_index("tile")
    per = LANES // rows
    n = per * rows
    row, column = iota((n, n), 0), iota((n, n), 1)
    same = row // rows == column // rows
    i, j = row % rows, column % rows
    dist = jnp.abs(i - j).astype(F32)
    left = (2 * (rows * tiles - rows * place) - 2 * jnp.maximum(i, j)).astype(F32)
    for g in range(levels // per):
        rate = jnp.concatenate(
            [jnp.broadcast_to(rate_ref[l : l + 1], (rows, LANES)) for l in range(g * per, (g + 1) * per)], axis=0
        )
        matrix = jnp.where(same, norm_of(rate) * jnp.exp(rate * dist) * (1.0 - jnp.exp(rate * left)), 0.0)
        for b in range(members):
            field = field_ref[b, g * per : (g + 1) * per].reshape(n, columns)
            out_ref[b, g * per : (g + 1) * per] = dot3(matrix, field).reshape(per, rows, columns)


def add_others(tiles, rate_ref, own_ref, received, out_ref, extra_ref=None):
    members, levels, rows, columns = own_ref.shape
    partner_ref, received = received[0], received[1:]
    place = lax.axis_index("tile")
    chip, upper, chips = place // 2, place % 2, tiles // 2
    rate = rate_ref[...]
    below = [jnp.where(upper == 1, partner_ref[0, b], 0.0) for b in range(members)]
    above = [jnp.where(upper == 0, partner_ref[1, b], 0.0) for b in range(members)]
    for k in range(1, chips):
        up = jnp.where(chip >= k, jnp.exp(rate * (rows * (2 * (k - 1) + upper)).astype(F32)), 0.0)
        down = jnp.where(chip < k, jnp.exp(rate * (rows * (2 * (chips - k) - 1 - upper)).astype(F32)), 0.0)
        for b in range(members):
            below[b] = below[b] + up * received[k - 1][b]
            above[b] = above[b] + down * received[k - 1][b]
    i = iota((rows, columns), 0)
    at = i.astype(F32)
    left = (2 * (rows * tiles - rows * place) - 2 * i).astype(F32)
    for l in range(levels):
        r = rate_ref[l : l + 1]
        from_below = jnp.exp(r * (at + 1.0)) * (1.0 - jnp.exp(r * left))
        from_above = jnp.exp(r * (rows - at))
        for b in range(members):
            total = own_ref[b, l] + (from_below * below[b][l : l + 1] + from_above * above[b][l : l + 1])
            out_ref[b, l] = total if extra_ref is None else total + extra_ref[b, l]


def indices(cells):
    whole = (cells + 0.5).astype(I32)
    return whole >> 7, whole & (LANES - 1)


def chunks_of(count):
    def run(body):
        def step(c, _):
            body(pl.ds(pl.multiple_of(c * 8, 8), 8))
            return 0

        lax.fori_loop(0, count // 8, step, 0, unroll=math.gcd(count // 8, 24))

    return run


def hot_rows(high, row_of, high_rows):
    count, _ = row_of.shape
    one, zero = jnp.ones((), BF16), jnp.zeros((), BF16)
    high = high.astype(F32)
    blocks = high_rows // count

    def rows(r):
        line = high[r : r + 1]
        return jnp.concatenate(
            [jnp.where(row_of == (line - float(count * h)).astype(BF16), one, zero) for h in range(blocks)], axis=0
        )

    return rows


def gather_kernel(tiles, per, rate_ref, own_ref, members_ref, *rest):
    received, rays = rest[: tiles // 2], rest[tiles // 2]
    out_ref, ray_ref, smooth_ref, table_ref = rest[tiles // 2 + 1 :]
    for s in range(tiles):
        for f in range(5):
            ray_ref[f, s * per : (s + 1) * per] = rays[s, f * per : (f + 1) * per]
    add_others(tiles, rate_ref, own_ref, received, smooth_ref)
    members, levels, rows, columns = own_ref.shape
    high_rows = levels * rows
    shares = []
    for f in range(2):
        share = jnp.zeros((high_rows, columns), F32)
        for b in range(members):
            share = share + members_ref[b, f].reshape(high_rows, columns).astype(F32) * smooth_ref[b].reshape(
                high_rows, columns
            )
        shares.append(share)
    largest = jnp.maximum(jnp.max(jnp.maximum(jnp.abs(shares[0]), jnp.abs(shares[1]))), 1e-30)
    scale, back = 256.0 / largest, largest * (1.0 / 256.0)
    for f in range(2):
        rest_of = shares[f].T * scale
        for k in range(PIECES):
            piece = rest_of.astype(F8)
            table_ref[(2 * k + f) * LANES : (2 * k + f + 1) * LANES] = piece
            rest_of = (rest_of - piece.astype(F32)) * 16.0
    row_of = iota((256, LANES), 0).astype(F32).astype(BF16)
    lane_of = iota((LANES, LANES), 0)

    @chunks_of(out_ref.shape[0])
    def _(at):
        high, low = indices(ray_ref[0, at, :])
        hot_row = hot_rows(high, row_of, high_rows)
        first, second = ray_ref[1, at, :] * back, ray_ref[2, at, :] * back
        lines = []
        for pair in range(4):
            hot = jnp.concatenate([hot_row(2 * pair), hot_row(2 * pair + 1)], axis=1).astype(F8)
            got = dot(table_ref[...], hot)
            total = got[: 2 * LANES]
            for k in range(1, PIECES):
                total = total + got[2 * k * LANES : 2 * (k + 1) * LANES] * 16.0**-k
            for h in range(2):
                r = 2 * pair + h
                here = lane_of == low[r : r + 1]
                part = total[:, h * LANES : (h + 1) * LANES]
                u = jnp.sum(jnp.where(here, part[:LANES], 0.0), axis=0, keepdims=True)
                v = jnp.sum(jnp.where(here, part[LANES:], 0.0), axis=0, keepdims=True)
                lines.append(u * first[r : r + 1] + v * second[r : r + 1])
        out_ref[at, :] = jnp.concatenate(lines, axis=0)


def scatter_kernel(tiles, blocks, rate_ref, high_ref, low_ref, members_ref, ray_ref, *rest):
    partial, (out_ref, state_ref, total_ref, mixed_ref, value_ref) = rest[:blocks], rest[blocks:]
    modelled = partial[0][...]
    for other in partial[1:]:
        modelled = modelled + other[...]
    departure = ray_ref[4] * (modelled - ray_ref[3])
    given = [ray_ref[1 + f] * departure for f in range(2)]
    largest = jnp.maximum(jnp.max(jnp.maximum(jnp.abs(given[0]), jnp.abs(given[1]))), 1e-30)
    scale, back = 256.0 / largest, largest * (1.0 / 256.0)
    for f in range(2):
        value_ref[f] = given[f] * scale
    members, levels, rows, columns = out_ref.shape
    high_rows = levels * rows
    row_of = iota((256, LANES), 0).astype(F32).astype(BF16)
    lane_of = iota((LANES, LANES), 0).astype(F32).astype(BF16)
    none = jnp.zeros((), BF16)
    total_ref[...] = jnp.zeros_like(total_ref)

    @chunks_of(ray_ref.shape[1])
    def _(at):
        high, low = indices(ray_ref[0, at, :])
        hot_row = hot_rows(high, row_of, high_rows)
        low = low.astype(F32)
        pieces = []
        rest_of = [value_ref[f, at, :] for f in range(2)]
        for _ in range(PIECES):
            for f in range(2):
                piece = rest_of[f].astype(F8).astype(F32)
                rest_of[f] = (rest_of[f] - piece) * 16.0
                pieces.append(piece)
        sides = []
        for r in range(8):
            here = lane_of == low[r : r + 1].astype(BF16)
            sides.append(
                jnp.concatenate(
                    [jnp.where(here, piece[r : r + 1].astype(BF16), none) for piece in pieces], axis=0
                ).astype(F8)
            )
        total_ref[...] += lax.dot_general(
            jnp.concatenate([hot_row(r).astype(F8) for r in range(8)], axis=1),
            jnp.concatenate(sides, axis=1),
            (((1,), (1,)), ((), ())),
            preferred_element_type=F32,
        )

    for l in range(levels):
        total = total_ref[l * rows : (l + 1) * rows]
        both = total[:, : 2 * LANES]
        for k in range(1, PIECES):
            both = both + total[:, 2 * k * LANES : 2 * (k + 1) * LANES] * 16.0**-k
        u, v = both[:, :LANES] * back, both[:, LANES:] * back
        for b in range(members):
            mixed_ref[b, l] = members_ref[b, 0, l].astype(F32) * u + members_ref[b, 1, l].astype(F32) * v
    filter_levels(mixed_ref, mixed_ref)
    filter_columns(mixed_ref, high_ref, low_ref, out_ref)
    states(tiles, rate_ref, out_ref, state_ref)


def last_kernel(tiles, rate_ref, alpha_ref, own_ref, *rest):
    add_others(tiles, rate_ref, own_ref, rest[:-1], rest[-1], alpha_ref)


def call(body, outs, scratch=(), cost=None, specs=None, params=PARAMS):
    def run(*args):
        return pl.pallas_call(
            body,
            out_shape=outs,
            in_specs=specs or [VMEM] * len(args),
            out_specs=jax.tree.map(lambda _: VMEM, outs),
            scratch_shapes=list(scratch),
            compiler_params=params,
            cost_estimate=cost,
        )(*args)

    return run


def shaped(*shape, dtype=F32):
    return jax.ShapeDtypeStruct(shape, dtype)


def over_members(part, blocks):
    return [lax.ppermute(part, "mem", [(i, i ^ k) for i in range(blocks)]) for k in range(1, blocks)]


def exchange(rate, own, rows, tiles):
    chips = tiles // 2
    partner = lax.ppermute(own, "tile", [(i, i ^ 1) for i in range(tiles)])
    given = call(functools.partial(chip_kernel, tiles, rows), [shaped(*own.shape[1:])] * (chips - 1))(
        rate, own, partner
    )
    return [
        partner,
        *(
            lax.ppermute(
                part, "tile", [(2 * c + h, 2 * ((c + k) % chips) + h) for c in range(chips) for h in range(2)]
            )
            for k, part in enumerate(given, 1)
        ),
    ]


def per_device(alpha, members, scales, observed, precision, ray_weights, cell_index, owner):
    tiles, blocks = lax.axis_size("tile"), lax.axis_size("mem")
    count_rays, gates = observed.shape
    capacity = 3 * count_rays // tiles
    per = capacity * (gates // LANES)
    shape = alpha.shape
    count, levels, rows, columns = shape
    anywhere = pl.BlockSpec(memory_space=pltpu.HBM)
    given = (
        owner.reshape(1, count_rays),
        scales.reshape(1, levels),
        cell_index,
        ray_weights,
        observed,
        precision,
    )
    sent, rate = call(
        functools.partial(pack_rays_kernel, per),
        [shaped(tiles, 5 * per, LANES), shaped(levels, LANES)],
        [*(pltpu.VMEM(x.shape, x.dtype) for x in given), pltpu.SemaphoreType.DMA((6,))],
        specs=[anywhere] * 6,
        params=WIDE,
    )(*given)
    here = lax.all_to_all(sent, "tile", split_axis=0, concat_axis=0, tiled=True)

    state = shaped(2, count, levels, columns)
    high, low, field, own = call(
        functools.partial(first_kernel, tiles),
        [shaped(levels, columns, columns, dtype=BF16)] * 2 + [shaped(*shape), state],
        [pltpu.VMEM(shape, F32)],
    )(rate, alpha)
    received = exchange(rate, own, rows, tiles)
    own = call(functools.partial(within_kernel, tiles), shaped(*shape))(rate, field)
    total = tiles * per
    modelled, ray = call(
        functools.partial(gather_kernel, tiles, per),
        [shaped(total, LANES), shaped(5, total, LANES)],
        [pltpu.VMEM(shape, F32), pltpu.VMEM((2 * PIECES * LANES, levels * rows), F8)],
        COST,
    )(rate, own, members, *received, here)
    field, own = call(
        functools.partial(scatter_kernel, tiles, blocks),
        [shaped(*shape), state],
        [
            pltpu.VMEM((levels * rows, 2 * PIECES * LANES), F32),
            pltpu.VMEM(shape, F32),
            pltpu.VMEM((2, total, LANES), F32),
        ],
        COST,
    )(rate, high, low, members, ray, modelled, *over_members(modelled, blocks))
    received = exchange(rate, own, rows, tiles)
    own = call(functools.partial(within_kernel, tiles), shaped(*shape))(rate, field)
    return call(functools.partial(last_kernel, tiles), shaped(*shape))(rate, alpha, own, *received)


def solution(mesh):
    return jax.shard_map(
        per_device,
        mesh=mesh,
        in_specs=(
            P("mem", None, "tile", None),
            P("mem", None, None, "tile", None),
            P(),
            P("tile", None),
            P("tile", None),
            P("tile", None, None),
            P("tile", None),
            P("tile", None),
        ),
        out_specs=P("mem", None, "tile", None),
        check_vma=False,
    )
```
